128 devices in a mesh: bin: 4 (over x_hi, core), slab: 32 (over z, x_lo, y).
Axes of the slice: x: 4 (x_hi: 2, x_lo: 2; x = x_hi * 2 + x_lo), y: 4, z: 4, core: 2. Of those that a mesh axis runs over, the one named last changes fastest.
Arguments:
- volumes: float32 [8, 128, 256, 512], P('bin', 'slab'), may hold values from -6 to 6
- attenuation: float32 [8, 3], replicated, may hold values from 0.2 to 1.2
- penalty: float32 [1], replicated, may hold values from 0.2 to 0.4
- tv_weight: float32 [1], replicated, may hold values from 0.3 to 0.8
Outputs:
- materials: float32 [3, 128, 256, 512], P(None, ('bin', 'slab'))
The draws below stay inside these ranges and needn't reach their ends.
All inputs are finite; a program needn't handle non-finite values.
Results may differ from the reference program's by a relative error of at most 0.0001.
Values sent between devices are 32-bit elements; how exact they have to be, the bound alone decides.
A program may use at most 64 MiB of HBM per device.

```python
import math
import jax
import jax.numpy as jnp
from jax import lax

BINS = 8
MATS = 3
NX = 512
ITERS = 3
NZ = 128
NY = 256


def block_levels(rng, shape, shards, least, largest):
    factor_of = 1.0
    for position, blocks in shards:
        heights = jax.random.uniform(jax.random.fold_in(jax.random.fold_in(rng, 6), position), (blocks,), jnp.float32, least / len(shards), largest / len(shards))
        factor_of = factor_of * jnp.repeat(jnp.exp(heights), shape[position] // blocks).reshape((-1,) + (1,) * (len(shape) - 1 - position))
    return factor_of


def bell_draw(own_key, shape, width, bound, cuts=(), kind=jnp.bfloat16):
    drawn = width * jax.random.normal(own_key, shape, jnp.float32)
    if cuts:
        drawn = drawn * block_levels(own_key, shape, cuts, -0.22, 0.18)
    return jnp.clip(drawn, -bound, bound).astype(kind)


def setup_inputs(seed: int = 0) -> dict:
    key_list = jax.random.split(jax.random.key(seed), 5)
    return {
        "volumes": bell_draw(key_list[0], (BINS, NZ, NY, NX), 1.0, 6.0, ((0, 4), (1, 32)), jnp.float32),
        "attenuation": jnp.clip(jax.random.uniform(key_list[1], (BINS, MATS), jnp.float32, 0.2, 1.2), 0.2, 1.2),
        "penalty": jnp.clip(jnp.exp(jax.random.uniform(key_list[2], (1,), jnp.float32, math.log(0.2), math.log(0.4))), 0.2, 0.4),
        "tv_weight": jnp.clip(jnp.exp(jax.random.uniform(key_list[3], (1,), jnp.float32, math.log(0.3), math.log(0.8))), 0.3, 0.8),
    }


def inverse_three(matrix):
    cofactor = [[matrix[(row + 1) % 3, (col + 1) % 3] * matrix[(row + 2) % 3, (col + 2) % 3] - matrix[(row + 1) % 3, (col + 2) % 3] * matrix[(row + 2) % 3, (col + 1) % 3] for col in range(3)] for row in range(3)]
    determinant = matrix[0, 0] * cofactor[0][0] + matrix[0, 1] * cofactor[0][1] + matrix[0, 2] * cofactor[0][2]
    return [[cofactor[col][row] / determinant for col in range(3)] for row in range(3)]

def normal_inverse(attenuation, penalty_value):
    gram = jnp.dot(attenuation.T, attenuation, precision=lax.Precision.HIGHEST)
    gram = gram + 12.0 * penalty_value * jnp.eye(3, dtype=jnp.float32)
    return inverse_three(gram)

def apply_inverse(inverse, fields):
    return jnp.stack([inverse[row][0] * fields[0] + inverse[row][1] * fields[1] + inverse[row][2] * fields[2] for row in range(3)])

def project(attenuation, volumes):
    return jnp.einsum('km,kzyx->mzyx', attenuation, volumes, precision=lax.Precision.HIGHEST)

def forward_diff(field, axis):
    count = field.shape[axis]
    upper = lax.slice_in_dim(field, 1, count, axis=axis)
    lower = lax.slice_in_dim(field, 0, count - 1, axis=axis)
    zeros = jnp.zeros_like(lax.slice_in_dim(field, 0, 1, axis=axis))
    return jnp.concatenate([upper - lower, zeros], axis)

def gradient(field):
    return [forward_diff(field, 1), forward_diff(field, 2), forward_diff(field, 3)]

def divergence(parts):
    total = jnp.zeros_like(parts[0])
    for axis, part in zip((1, 2, 3), parts):
        count = part.shape[axis]
        earlier = jnp.concatenate([jnp.zeros_like(lax.slice_in_dim(part, 0, 1, axis=axis)), lax.slice_in_dim(part, 0, count - 1, axis=axis)], axis)
        total = total + (part - earlier)
    return total

def clip_group(parts, threshold):
    squares = lax.optimization_barrier(jnp.sum(parts[0] * parts[0], axis=0)) + lax.optimization_barrier(jnp.sum(parts[1] * parts[1], axis=0)) + lax.optimization_barrier(jnp.sum(parts[2] * parts[2], axis=0))
    scale = threshold / jnp.maximum(jnp.sqrt(squares), threshold)
    return [part * scale[None] for part in parts]

def reference(volumes, attenuation, penalty, tv_weight):
    penalty_value = penalty[0]
    threshold = tv_weight[0] / penalty_value
    inverse = normal_inverse(attenuation, penalty_value)
    data = project(attenuation, volumes)
    field = apply_inverse(inverse, data)
    dual = clip_group(gradient(field), threshold)
    step_parts = [2.0 * part for part in dual]
    for turn in range(ITERS):
        field = apply_inverse(inverse, data + 12.0 * penalty_value * field + penalty_value * divergence(step_parts))
        if turn < ITERS - 1:
            grads = gradient(field)
            fresh = clip_group([grads[index] + dual[index] for index in range(3)], threshold)
            step_parts = [2.0 * fresh[index] - dual[index] for index in range(3)]
            dual = fresh
    return field
```

```python
import jax
import jax.numpy as jnp
from jax import lax
from jax.experimental import pallas as pl
from jax.experimental.pallas import tpu as pltpu
from jax.sharding import PartitionSpec as P

MESH = pl.DeviceIdType.MESH
F32 = jnp.float32
HALO = 3
LAYERS = 16 + 2 * HALO
NX = 512


def position():
    bin_index = lax.axis_index("bin")
    slab_index = lax.axis_index("slab")
    return (
        bin_index // 2,
        bin_index % 2,
        slab_index // 16,
        (slab_index // 8) % 2,
        (slab_index // 4) % 2,
        slab_index % 4,
    )


def device(xh, core, pz1, pz0, xl, py):
    return (xh * 2 + core, pz1 * 16 + pz0 * 8 + xl * 4 + py)


def block_device(zb, yb):
    return device(zb // 4, yb % 2, yb // 8, (zb // 2) % 2, zb % 2, (yb // 2) % 4)


def scalars(att, penalty, tv_weight, xh):
    rho = penalty[0]
    threshold = tv_weight[0] / rho
    gram = [[None] * 3 for _ in range(3)]
    for i in range(3):
        for j in range(i, 3):
            total = att[0, i] * att[0, j]
            for k in range(1, 8):
                total = total + att[k, i] * att[k, j]
            gram[i][j] = gram[j][i] = total + 12.0 * rho if i == j else total
    cofactor = [
        [
            gram[(r + 1) % 3][(c + 1) % 3] * gram[(r + 2) % 3][(c + 2) % 3]
            - gram[(r + 1) % 3][(c + 2) % 3] * gram[(r + 2) % 3][(c + 1) % 3]
            for c in range(3)
        ]
        for r in range(3)
    ]
    determinant = sum(gram[0][c] * cofactor[0][c] for c in range(3))
    inverse = [[cofactor[c][r] / determinant for c in range(3)] for r in range(3)]
    weight = [
        [sum(inverse[m][n] * att[4 * xh + k, n] for n in range(3)) for k in range(4)]
        for m in range(3)
    ]
    scaled = [[rho * inverse[m][n] for n in range(3)] for m in range(3)]
    return threshold, weight, scaled


def kernel(
    vol, att, penalty, tv_weight, out,
    raw, part, passed, landed, base, field, dual, carry,
    pack_lo, pack_hi, got_lo, got_hi, result,
    load_sem, core_send, core_recv, one_send, one_recv, two_send, two_recv,
    hz_send, hz_recv, hy_send, hy_recv, out_send, out_recv,
):
    xh, core, pz1, pz0, xl, py = position()
    zb = xh * 4 + pz0 * 2 + xl
    yb = pz1 * 8 + py * 2 + core
    partner = device(xh, 1 - core, pz1, pz0, xl, py)
    across = device(xh, core, 1 - pz1, pz0, xl, py)

    def load(q):
        return pltpu.make_async_copy(
            vol.at[:, :, q, core], raw.at[pl.ds(core * 2, 2), :, q], load_sem.at[q]
        )

    def load_body(q, _):
        load(q).start()
        return 0

    lax.fori_loop(0, 8, load_body, 0)

    barrier = pltpu.get_barrier_semaphore()

    def greet(target):
        pl.semaphore_signal(barrier, inc=1, device_id=target, device_id_type=MESH)

    greet(partner)
    greet(across)
    for side in range(2):
        for row in range(4):
            target = device(side, core, pz1, pz0, xl, row)

            @pl.when(jnp.logical_or(side != xh, row != py))
            def _():
                greet(target)

    for dz in (1, 7):
        greet(block_device((zb + dz) % 8, yb))
    for dy in (1, 15):
        greet(block_device(zb, (yb + dy) % 16))

    home = jnp.logical_and(pz0 == core, pz1 == xl)

    def greet_body(y, _):
        source = device(xh, y % 2, y // 8, core, pz1, (y // 2) % 4)

        @pl.when(jnp.logical_not(jnp.logical_and(home, y == yb)))
        def _():
            greet(source)

        return 0

    lax.fori_loop(0, 16, greet_body, 0)

    threshold, weight, scaled = scalars(att, penalty, tv_weight, xh)

    @pl.when(zb == 0)
    def _():
        base[pl.ds(0, HALO)] = jnp.zeros((HALO, 3, 24, NX), F32)

    @pl.when(zb == 7)
    def _():
        base[pl.ds(16 + HALO, HALO)] = jnp.zeros((HALO, 3, 24, NX), F32)

    @pl.when(yb == 0)
    def _():
        got_lo[...] = jnp.zeros_like(got_lo)

    @pl.when(yb == 15)
    def _():
        got_hi[...] = jnp.zeros_like(got_hi)

    pl.semaphore_wait(barrier, 2 + 7 + 4 + 16 - jnp.where(home, 1, 0))

    def swap(q):
        return pltpu.make_async_remote_copy(
            src_ref=vol.at[:, :, q, 1 - core],
            dst_ref=raw.at[pl.ds(core * 2, 2), :, q],
            send_sem=core_send.at[q],
            recv_sem=core_recv.at[q],
            device_id=partner,
            device_id_type=MESH,
        )

    def order(i):
        far = i // 4
        return (far ^ (1 - pz1)) * 4 + (py + i) % 4

    def swap_body(i, _):
        swap(order(i)).start()
        return 0

    lax.fori_loop(0, 8, swap_body, 0)

    def project(q):
        load(q).wait()
        swap(q).wait_recv()

        def body(j, _):
            for r in range(2):
                rows = pl.ds(8 * r, 8)
                bins = [raw[k, j, q, rows, :] for k in range(4)]
                for m in range(3):
                    part[q, j // 2, m, j % 2, rows, :] = (
                        weight[m][0] * bins[0]
                        + weight[m][1] * bins[1]
                        + weight[m][2] * bins[2]
                        + weight[m][3] * bins[3]
                    )
            return 0

        lax.fori_loop(0, 4, body, 0)

    def one(row, h):
        return pltpu.make_async_remote_copy(
            src_ref=part.at[(1 - pz1) * 4 + row, h],
            dst_ref=passed.at[row, h],
            send_sem=one_send.at[row * 2 + h],
            recv_sem=one_recv.at[row * 2 + h],
            device_id=across,
            device_id_type=MESH,
        )

    def one_body(i, _):
        row = (py + i) % 4
        project((1 - pz1) * 4 + row)
        for h in range(2):
            one(row, h).start()
        return 0

    lax.fori_loop(0, 4, one_body, 0)

    def two(source, side, row, h, at):
        return pltpu.make_async_remote_copy(
            src_ref=source,
            dst_ref=landed.at[xh, py, h],
            send_sem=two_send.at[at],
            recv_sem=two_recv.at[xh * 8 + py * 2 + h],
            device_id=device(side, core, pz1, pz0, xl, row),
            device_id_type=MESH,
        )

    def two_local(source, h):
        return pltpu.make_async_copy(
            source, landed.at[xh, py, h], two_recv.at[xh * 8 + py * 2 + h]
        )

    def two_start(source, side, row, h, at):
        mine = jnp.logical_and(side == xh, row == py)

        @pl.when(mine)
        def _():
            two_local(source, h).start()

        @pl.when(jnp.logical_not(mine))
        def _():
            two(source, side, row, h, at).start()

    def own_body(i, _):
        row = (py + i) % 4
        project(pz1 * 4 + row)
        for h in range(2):
            two_start(part.at[pz1 * 4 + row, h], pz1, row, h, row * 2 + h)
        return 0

    lax.fori_loop(0, 4, own_body, 0)

    def pass_body(i, _):
        row = (py + i // 2) % 4
        h = i % 2
        one(row, h).wait_recv()
        two_start(passed.at[row, h], 1 - pz1, row, h, 8 + row * 2 + h)
        return 0

    lax.fori_loop(0, 8, pass_body, 0)

    def reduce_body(i, _):
        row = (py + 4 - i // 2) % 4
        h = i % 2
        for side in range(2):
            pltpu.make_async_remote_copy(
                src_ref=landed.at[side, row, h],
                dst_ref=landed.at[side, row, h],
                send_sem=two_send.at[0],
                recv_sem=two_recv.at[side * 8 + row * 2 + h],
                device_id=partner,
                device_id_type=MESH,
            ).wait_recv()
        for jj in range(2):
            layer = HALO + row * 4 + h * 2 + jj
            for m in range(3):
                base[layer, m, pl.ds(0, 16), :] = (
                    landed[0, row, h, m, jj] + landed[1, row, h, m, jj]
                )
        return 0

    lax.fori_loop(0, 8, reduce_body, 0)

    below = block_device((zb + 7) % 8, yb)
    above = block_device((zb + 1) % 8, yb)
    before = block_device(zb, (yb + 15) % 16)
    after = block_device(zb, (yb + 1) % 16)

    def halo_z(which):
        first, target, place = ((HALO, below, 16 + HALO), (16, above, 0))[which]
        return pltpu.make_async_remote_copy(
            src_ref=base.at[pl.ds(first, HALO), :, pl.ds(0, 16)],
            dst_ref=base.at[pl.ds(place, HALO), :, pl.ds(0, 16)],
            send_sem=hz_send.at[which],
            recv_sem=hz_recv.at[which],
            device_id=target,
            device_id_type=MESH,
        )

    def halo_y(which, late):
        pack, got, target = ((pack_lo, got_hi, before), (pack_hi, got_lo, after))[which]
        rows = pl.ds(8, 3) if late else pl.ds(0, 8)
        return pltpu.make_async_remote_copy(
            src_ref=pack.at[rows],
            dst_ref=got.at[rows],
            send_sem=hy_send.at[which + 2 * late],
            recv_sem=hy_recv.at[which + 2 * late],
            device_id=target,
            device_id_type=MESH,
        )

    has_below, has_above = zb > 0, zb < 7
    has_before, has_after = yb > 0, yb < 15

    @pl.when(has_below)
    def _():
        halo_z(0).start()

    @pl.when(has_above)
    def _():
        halo_z(1).start()

    sub = lax.broadcasted_iota(jnp.int32, (8, NX), 0)

    def pair(i, late):
        return (i, i + 19) if late else (i + HALO, i + HALO + 8)

    def pack_pair(i, late):
        first, second = pair(i, late)
        at = i + 8 if late else i
        for m in range(3):
            lo_first = base[first, m, pl.ds(0, 8), :]
            lo_second = pltpu.roll(base[second, m, pl.ds(0, 8), :], 4, 0)
            pack_lo[at, m] = jnp.where(sub < 4, lo_first, lo_second)
            hi_first = base[first, m, pl.ds(8, 8), :]
            hi_second = pltpu.roll(base[second, m, pl.ds(8, 8), :], 4, 0)
            pack_hi[at, m] = jnp.where(sub < 4, hi_second, hi_first)

    def unpack_pair(i, late):
        first, second = pair(i, late)
        at = i + 8 if late else i
        for m in range(3):
            lo = got_lo[at, m]
            hi = got_hi[at, m]
            base[first, m, pl.ds(16, 8), :] = jnp.where(sub < 4, hi, lo)
            base[second, m, pl.ds(16, 8), :] = pltpu.roll(jnp.where(sub < 4, lo, hi), 4, 0)

    def each_pair(work, late):
        def body(i, _):
            work(i, late)
            return 0

        lax.fori_loop(0, 3 if late else 8, body, 0)

    each_pair(pack_pair, False)

    @pl.when(has_before)
    def _():
        halo_y(0, 0).start()

    @pl.when(has_after)
    def _():
        halo_y(1, 0).start()

    @pl.when(has_above)
    def _():
        halo_z(0).wait_recv()

    @pl.when(has_below)
    def _():
        halo_z(1).wait_recv()

    each_pair(pack_pair, True)

    @pl.when(has_before)
    def _():
        halo_y(0, 1).start()

    @pl.when(has_after)
    def _():
        halo_y(1, 1).start()

    for late in range(2):
        @pl.when(has_after)
        def _():
            halo_y(0, late).wait_recv()

        @pl.when(has_before)
        def _():
            halo_y(1, late).wait_recv()

        each_pair(unpack_pair, late == 1)

    lane = lax.broadcasted_iota(jnp.int32, (8, NX), 1)
    x_mask = jnp.where(lane == NX - 1, 0.0, 1.0).astype(F32)
    y_mask = {
        1: jnp.where(jnp.logical_and(sub == 7, yb == 15), 0.0, 1.0).astype(F32),
        2: jnp.where(jnp.logical_and(sub == 7, yb == 0), 0.0, 1.0).astype(F32),
    }
    limit = threshold * threshold

    def sweep(turn):
        src = base if turn == 0 else field

        def body(z, _):
            z_global = zb * 16 + z - HALO
            z_mask = jnp.where(
                jnp.logical_or(z_global == 127, z_global == -1), 0.0, 1.0
            ).astype(F32)
            here = [[src[z, m, pl.ds(8 * t, 8), :] for m in range(3)] for t in range(3)]
            rolled = [[pltpu.roll(here[t][m], 7, 0) for m in range(3)] for t in range(3)]

            def steps(t):
                rows = pl.ds(8 * t, 8)
                values, old, squares = [], [], None
                for m in range(3):
                    f = here[t][m]
                    along_z = (src[z + 1, m, rows, :] - f) * z_mask
                    along_y = jnp.where(sub == 7, rolled[(t + 1) % 3][m], rolled[t][m]) - f
                    if t:
                        along_y = along_y * y_mask[t]
                    along_x = (pltpu.roll(f, NX - 1, 1) - f) * x_mask
                    triple = [along_z, along_y, along_x]
                    if turn:
                        past = [dual[z, 3 * m + d, rows, :] for d in range(3)]
                        triple = [a + b for a, b in zip(triple, past)]
                        old.append(past)
                    values.append(triple)
                    for v in triple:
                        squares = v * v if squares is None else squares + v * v
                scale = threshold * lax.rsqrt(jnp.maximum(squares, limit))
                twice = scale + scale
                moved = []
                for m in range(3):
                    if turn < 2:
                        for d in range(3):
                            dual[z, 3 * m + d, rows, :] = values[m][d] * scale
                    triple = [v * twice for v in values[m]]
                    if turn:
                        triple = [a - b for a, b in zip(triple, old[m])]
                    moved.append(triple)
                return moved

            def inner(t, moved):
                rows = pl.ds(8 * t, 8)
                partial, turned = [], []
                for m in range(3):
                    step_z, step_y, step_x = moved[m]
                    total = step_z - carry[m, rows, :]
                    carry[m, rows, :] = step_z
                    total = total + (step_x - pltpu.roll(step_x, 1, 1)) + step_y
                    partial.append(total + 12.0 * here[t][m])
                    turned.append(pltpu.roll(step_y, 1, 0))
                return partial, turned

            def finish(t, partial, own, earlier):
                rows = pl.ds(8 * t, 8)
                total = [
                    partial[m] - jnp.where(sub == 0, earlier[m], own[m]) for m in range(3)
                ]
                for m in range(3):
                    value = (
                        base[z, m, rows, :]
                        + scaled[m][0] * total[0]
                        + scaled[m][1] * total[1]
                        + scaled[m][2] * total[2]
                    )
                    if turn < 2:
                        field[z, m, rows, :] = value
                    else:
                        result[z - 2, m, rows, :] = value

            moved = steps(2)
            if turn < 2:
                partial_two, turned_two = inner(2, moved)
            else:
                turned_two = [pltpu.roll(moved[m][1], 1, 0) for m in range(3)]
            partial, turned_zero = inner(0, steps(0))
            finish(0, partial, turned_zero, turned_two)
            partial, turned_one = inner(1, steps(1))
            finish(1, partial, turned_one, turned_zero)
            if turn < 2:
                finish(2, partial_two, turned_two, turned_one)
            return 0

        lax.fori_loop(turn, LAYERS - 1 - turn, body, 0)

    for turn in range(3):
        sweep(turn)

    def send(layer):
        return pltpu.make_async_remote_copy(
            src_ref=result.at[1 + layer],
            dst_ref=out.at[:, pl.ds(pl.multiple_of(yb * 16, 16), 16)],
            send_sem=out_send.at[layer],
            recv_sem=out_recv.at[yb],
            device_id=(xh * 2 + pz0, xl * 16 + layer),
            device_id_type=MESH,
        )

    own_layer = pz0 * 8 + xl * 4 + py

    def send_body(i, _):
        layer = (i + py) % 4 + 4 * ((i // 4) ^ (xl + 2 * pz0))
        mine = jnp.logical_and(home, layer == own_layer)

        @pl.when(mine)
        def _():
            pltpu.make_async_copy(
                result.at[1 + layer],
                out.at[:, pl.ds(pl.multiple_of(yb * 16, 16), 16)],
                out_recv.at[yb],
            ).start()

        @pl.when(jnp.logical_not(mine))
        def _():
            send(layer).start()

        return 0

    lax.fori_loop(0, 16, send_body, 0)

    def drain_swap(q, _):
        swap(q).wait_send()
        one(q // 2, q % 2).wait_send()
        return 0

    lax.fori_loop(0, 8, drain_swap, 0)

    def drain_two(i, _):
        far = i // 8
        row, h = (i // 2) % 4, i % 2
        side = far ^ pz1

        @pl.when(jnp.logical_not(jnp.logical_and(side == xh, row == py)))
        def _():
            two(passed.at[row, h], side, row, h, i).wait_send()

        return 0

    lax.fori_loop(0, 16, drain_two, 0)

    for which in range(2):
        @pl.when((has_below, has_above)[which])
        def _():
            halo_z(which).wait_send()

        @pl.when((has_before, has_after)[which])
        def _():
            halo_y(which, 0).wait_send()
            halo_y(which, 1).wait_send()

    def drain_out(i, _):
        @pl.when(jnp.logical_not(jnp.logical_and(home, i == own_layer)))
        def _():
            send(i).wait_send()

        pltpu.make_async_remote_copy(
            src_ref=result.at[0],
            dst_ref=out.at[:, pl.ds(pl.multiple_of(i * 16, 16), 16)],
            send_sem=out_send.at[0],
            recv_sem=out_recv.at[i],
            device_id=partner,
            device_id_type=MESH,
        ).wait_recv()
        return 0

    lax.fori_loop(0, 16, drain_out, 0)


def on_device(volumes, attenuation, penalty, tv_weight):
    vol = volumes.reshape(2, 4, 8, 2, 16, NX)
    dma = pltpu.SemaphoreType.DMA
    out = pl.pallas_call(
        kernel,
        out_shape=jax.ShapeDtypeStruct((3, 256, NX), F32),
        in_specs=[pl.BlockSpec(memory_space=pl.ANY)]
        + [pl.BlockSpec(memory_space=pltpu.SMEM)] * 3,
        out_specs=pl.BlockSpec(memory_space=pl.ANY),
        scratch_shapes=[
            pltpu.VMEM((4, 4, 8, 16, NX), F32),
            pltpu.VMEM((8, 2, 3, 2, 16, NX), F32),
            pltpu.VMEM((4, 2, 3, 2, 16, NX), F32),
            pltpu.VMEM((2, 4, 2, 3, 2, 16, NX), F32),
            pltpu.VMEM((LAYERS, 3, 24, NX), F32),
            pltpu.VMEM((LAYERS, 3, 24, NX), F32),
            pltpu.VMEM((LAYERS, 9, 24, NX), F32),
            pltpu.VMEM((3, 24, NX), F32),
            pltpu.VMEM((11, 3, 8, NX), F32),
            pltpu.VMEM((11, 3, 8, NX), F32),
            pltpu.VMEM((11, 3, 8, NX), F32),
            pltpu.VMEM((11, 3, 8, NX), F32),
            pltpu.VMEM((17, 3, 16, NX), F32),
            dma((8,)), dma((8,)), dma((8,)),
            dma((8,)), dma((8,)),
            dma((16,)), dma((16,)),
            dma((2,)), dma((2,)), dma((4,)), dma((4,)),
            dma((16,)), dma((16,)),
        ],
        compiler_params=pltpu.CompilerParams(
            collective_id=0, has_side_effects=True, vmem_limit_bytes=56 * 1024 * 1024
        ),
        cost_estimate=pl.CostEstimate(
            flops=60_000_000, bytes_accessed=8_000_000, transcendentals=400_000
        ),
    )(vol, attenuation, penalty, tv_weight)
    return out.reshape(3, 1, 256, NX)


def solution(mesh):
    placed = (P("bin", "slab", None, None), P(), P(), P())
    return jax.shard_map(
        on_device,
        mesh=mesh,
        in_specs=placed,
        out_specs=P(None, ("bin", "slab"), None, None),
        check_vma=False,
    )
```

```python
import jax
import jax.numpy as jnp
from jax import lax
from jax.experimental import pallas as pl
from jax.experimental.pallas import tpu as pltpu
from jax.sharding import PartitionSpec as P

MESH = pl.DeviceIdType.MESH
F32 = jnp.float32
HALO = 3
LAYERS = 16 + 2 * HALO
NX = 512
LAG = 4
PIECES = 16


def position():
    bin_index = lax.axis_index("bin")
    slab_index = lax.axis_index("slab")
    return (
        bin_index // 2,
        bin_index % 2,
        slab_index // 16,
        (slab_index // 8) % 2,
        (slab_index // 4) % 2,
        slab_index % 4,
    )


def device(xh, core, pz1, pz0, xl, py):
    return (xh * 2 + core, pz1 * 16 + pz0 * 8 + xl * 4 + py)


def block_device(zb, yb):
    return device(zb // 4, yb % 2, yb // 8, (zb // 2) % 2, zb % 2, (yb // 2) % 4)


def scalars(att, penalty, tv_weight, xh):
    rho = penalty[0]
    threshold = tv_weight[0] / rho
    gram = [[None] * 3 for _ in range(3)]
    for i in range(3):
        for j in range(i, 3):
            total = att[0, i] * att[0, j]
            for k in range(1, 8):
                total = total + att[k, i] * att[k, j]
            gram[i][j] = gram[j][i] = total + 12.0 * rho if i == j else total
    cofactor = [
        [
            gram[(r + 1) % 3][(c + 1) % 3] * gram[(r + 2) % 3][(c + 2) % 3]
            - gram[(r + 1) % 3][(c + 2) % 3] * gram[(r + 2) % 3][(c + 1) % 3]
            for c in range(3)
        ]
        for r in range(3)
    ]
    determinant = sum(gram[0][c] * cofactor[0][c] for c in range(3))
    inverse = [[cofactor[c][r] / determinant for c in range(3)] for r in range(3)]
    weight = [
        [sum(inverse[m][n] * att[4 * xh + k, n] for n in range(3)) for k in range(4)]
        for m in range(3)
    ]
    scaled = [[rho * inverse[m][n] for n in range(3)] for m in range(3)]
    return threshold, weight, scaled


def kernel(
    vol, att, penalty, tv_weight, out,
    raw, part, passed, landed, base, field, dual, carry,
    pack_lo, pack_hi, got_lo, got_hi, result,
    load_sem, core_send, core_recv, one_send, one_recv, two_send, two_recv,
    hz_send, hz_recv, hy_send, hy_recv, out_send, out_recv,
):
    xh, core, pz1, pz0, xl, py = position()
    zb = xh * 4 + pz0 * 2 + xl
    yb = pz1 * 8 + py * 2 + core
    partner = device(xh, 1 - core, pz1, pz0, xl, py)
    across = device(xh, core, 1 - pz1, pz0, xl, py)

    def bins_at(n):
        return n // 2, pl.ds(((1 - n % 2) ^ pz1) * 4, 4)

    def load(n):
        layer, rows = bins_at(n)
        return pltpu.make_async_copy(
            vol.at[:, layer, rows, core], raw.at[pl.ds(core * 2, 2), layer, rows], load_sem.at[n]
        )

    def load_body(n, _):
        load(n).start()
        return 0

    lax.fori_loop(0, 8, load_body, 0)

    barrier = pltpu.get_barrier_semaphore()

    def greet(target):
        pl.semaphore_signal(barrier, inc=1, device_id=target, device_id_type=MESH)

    greet(partner)
    greet(across)
    for side in range(2):
        for row in range(4):
            target = device(side, core, pz1, pz0, xl, row)

            @pl.when(jnp.logical_or(side != xh, row != py))
            def _():
                greet(target)

    for dz in (1, 7):
        greet(block_device((zb + dz) % 8, yb))
    for dy in (1, 15):
        greet(block_device(zb, (yb + dy) % 16))

    home = jnp.logical_and(pz0 == core, pz1 == xl)

    def greet_body(y, _):
        source = device(xh, y % 2, y // 8, core, pz1, (y // 2) % 4)

        @pl.when(jnp.logical_not(jnp.logical_and(home, y == yb)))
        def _():
            greet(source)

        return 0

    lax.fori_loop(0, 16, greet_body, 0)

    threshold, weight, scaled = scalars(att, penalty, tv_weight, xh)

    @pl.when(zb == 0)
    def _():
        base[pl.ds(0, HALO)] = jnp.zeros((HALO, 3, 24, NX), F32)

    @pl.when(zb == 7)
    def _():
        base[pl.ds(16 + HALO, HALO)] = jnp.zeros((HALO, 3, 24, NX), F32)

    @pl.when(yb == 0)
    def _():
        got_lo[...] = jnp.zeros_like(got_lo)

    @pl.when(yb == 15)
    def _():
        got_hi[...] = jnp.zeros_like(got_hi)

    pl.semaphore_wait(barrier, 2 + 7 + 4 + 16 - jnp.where(home, 1, 0))

    def swap(n):
        layer, rows = bins_at(n)
        return pltpu.make_async_remote_copy(
            src_ref=vol.at[:, layer, rows, 1 - core],
            dst_ref=raw.at[pl.ds(core * 2, 2), layer, rows],
            send_sem=core_send.at[n],
            recv_sem=core_recv.at[n],
            device_id=partner,
            device_id_type=MESH,
        )

    def swap_body(n, _):
        swap(n).start()
        return 0

    lax.fori_loop(0, 4, swap_body, 0)

    def project(n):
        load(n).wait()
        swap(n).wait_recv()

        @pl.when(n < 4)
        def _():
            swap(n + 4).start()

        layer = n // 2
        first = ((1 - n % 2) ^ pz1) * 4

        def body(k, _):
            q = first + k
            for r in range(2):
                rows = pl.ds(8 * r, 8)
                bins = [raw[b, layer, q, rows, :] for b in range(4)]
                for m in range(3):
                    part[q, layer, m, rows, :] = (
                        weight[m][0] * bins[0]
                        + weight[m][1] * bins[1]
                        + weight[m][2] * bins[2]
                        + weight[m][3] * bins[3]
                    )
            return 0

        lax.fori_loop(0, 4, body, 0)

    def ahead(i):
        k = i % 4
        return jnp.where(k < 2, 2 * k + 1, 6 - 2 * k)

    def piece(i):
        return (py + ahead(i)) % 4, i // 4

    def one(i):
        row, h = piece(i)
        return pltpu.make_async_remote_copy(
            src_ref=part.at[(1 - pz1) * 4 + row, h],
            dst_ref=passed.at[row, h],
            send_sem=one_send.at[i],
            recv_sem=one_recv.at[i],
            device_id=across,
            device_id_type=MESH,
        )

    def two(i, passing):
        row, h = piece(i)
        source = passed.at[row, h] if passing else part.at[pz1 * 4 + row, h]
        return pltpu.make_async_remote_copy(
            src_ref=source,
            dst_ref=landed.at[xh, py, h],
            send_sem=two_send.at[i + PIECES * passing],
            recv_sem=two_recv.at[(xh * 4 + py) * 4 + h],
            device_id=device(1 - pz1 if passing else pz1, core, pz1, pz0, xl, row),
            device_id_type=MESH,
        )

    def two_stays(i, passing):
        return jnp.logical_and(xh == (1 - pz1 if passing else pz1), ahead(i) == 0)

    def two_start(i, passing):
        row, h = piece(i)
        stays = two_stays(i, passing)
        source = passed.at[row, h] if passing else part.at[pz1 * 4 + row, h]

        @pl.when(stays)
        def _():
            pltpu.make_async_copy(
                source, landed.at[xh, py, h], two_recv.at[(xh * 4 + py) * 4 + h]
            ).start()

        @pl.when(jnp.logical_not(stays))
        def _():
            two(i, passing).start()

    def two_sent(i, passing):
        @pl.when(jnp.logical_not(two_stays(i, passing)))
        def _():
            two(i, passing).wait_send()

    def pass_on(i):
        one(i).wait_recv()
        two_start(i, 1)

    def input_body(i, _):
        @pl.when(i % 4 == 0)
        def _():
            project(i // 2)
            project(i // 2 + 1)

        one(i).start()
        two_start(i, 0)

        @pl.when(i >= LAG)
        def _():
            pass_on(i - LAG)

        return 0

    lax.fori_loop(0, PIECES, input_body, 0)

    def tail_body(i, _):
        pass_on(i)
        return 0

    lax.fori_loop(PIECES - LAG, PIECES, tail_body, 0)

    def reduce_body(i, _):
        row = (py + 4 - ahead(i)) % 4
        h = i // 4
        for side in range(2):
            pltpu.make_async_remote_copy(
                src_ref=landed.at[side, row, h],
                dst_ref=landed.at[side, row, h],
                send_sem=two_send.at[0],
                recv_sem=two_recv.at[(side * 4 + row) * 4 + h],
                device_id=partner,
                device_id_type=MESH,
            ).wait_recv()
        layer = HALO + row * 4 + h
        for m in range(3):
            base[layer, m, pl.ds(0, 16), :] = landed[0, row, h, m] + landed[1, row, h, m]
        return 0

    lax.fori_loop(0, PIECES, reduce_body, 0)

    below = block_device((zb + 7) % 8, yb)
    above = block_device((zb + 1) % 8, yb)
    before = block_device(zb, (yb + 15) % 16)
    after = block_device(zb, (yb + 1) % 16)

    def halo_z(which):
        first, target, place = ((HALO, below, 16 + HALO), (16, above, 0))[which]
        return pltpu.make_async_remote_copy(
            src_ref=base.at[pl.ds(first, HALO), :, pl.ds(0, 16)],
            dst_ref=base.at[pl.ds(place, HALO), :, pl.ds(0, 16)],
            send_sem=hz_send.at[which],
            recv_sem=hz_recv.at[which],
            device_id=target,
            device_id_type=MESH,
        )

    def halo_y(which, late):
        pack, got, target = ((pack_lo, got_hi, before), (pack_hi, got_lo, after))[which]
        rows = pl.ds(8, 3) if late else pl.ds(0, 8)
        return pltpu.make_async_remote_copy(
            src_ref=pack.at[rows],
            dst_ref=got.at[rows],
            send_sem=hy_send.at[which + 2 * late],
            recv_sem=hy_recv.at[which + 2 * late],
            device_id=target,
            device_id_type=MESH,
        )

    has_below, has_above = zb > 0, zb < 7
    has_before, has_after = yb > 0, yb < 15

    @pl.when(has_below)
    def _():
        halo_z(0).start()

    @pl.when(has_above)
    def _():
        halo_z(1).start()

    sub = lax.broadcasted_iota(jnp.int32, (8, NX), 0)

    def pair(i, late):
        return (i, i + 19) if late else (i + HALO, i + HALO + 8)

    def pack_pair(i, late):
        first, second = pair(i, late)
        at = i + 8 if late else i
        for m in range(3):
            lo_first = base[first, m, pl.ds(0, 8), :]
            lo_second = pltpu.roll(base[second, m, pl.ds(0, 8), :], 4, 0)
            pack_lo[at, m] = jnp.where(sub < 4, lo_first, lo_second)
            hi_first = base[first, m, pl.ds(8, 8), :]
            hi_second = pltpu.roll(base[second, m, pl.ds(8, 8), :], 4, 0)
            pack_hi[at, m] = jnp.where(sub < 4, hi_second, hi_first)

    def unpack_pair(i, late):
        first, second = pair(i, late)
        at = i + 8 if late else i
        for m in range(3):
            lo = got_lo[at, m]
            hi = got_hi[at, m]
            base[first, m, pl.ds(16, 8), :] = jnp.where(sub < 4, hi, lo)
            base[second, m, pl.ds(16, 8), :] = pltpu.roll(jnp.where(sub < 4, lo, hi), 4, 0)

    def each_pair(work, late):
        def body(i, _):
            work(i, late)
            return 0

        lax.fori_loop(0, 3 if late else 8, body, 0)

    each_pair(pack_pair, False)

    @pl.when(has_before)
    def _():
        halo_y(0, 0).start()

    @pl.when(has_after)
    def _():
        halo_y(1, 0).start()

    @pl.when(has_above)
    def _():
        halo_z(0).wait_recv()

    @pl.when(has_below)
    def _():
        halo_z(1).wait_recv()

    each_pair(pack_pair, True)

    @pl.when(has_before)
    def _():
        halo_y(0, 1).start()

    @pl.when(has_after)
    def _():
        halo_y(1, 1).start()

    for late in range(2):
        @pl.when(has_after)
        def _():
            halo_y(0, late).wait_recv()

        @pl.when(has_before)
        def _():
            halo_y(1, late).wait_recv()

        each_pair(unpack_pair, late == 1)

    lane = lax.broadcasted_iota(jnp.int32, (8, NX), 1)
    x_mask = jnp.where(lane == NX - 1, 0.0, 1.0).astype(F32)
    y_mask = {
        1: jnp.where(jnp.logical_and(sub == 7, yb == 15), 0.0, 1.0).astype(F32),
        2: jnp.where(jnp.logical_and(sub == 7, yb == 0), 0.0, 1.0).astype(F32),
    }
    limit = threshold * threshold

    def sweep(turn):
        src = base if turn == 0 else field

        def body(z, _):
            z_global = zb * 16 + z - HALO
            z_mask = jnp.where(
                jnp.logical_or(z_global == 127, z_global == -1), 0.0, 1.0
            ).astype(F32)
            here = [[src[z, m, pl.ds(8 * t, 8), :] for m in range(3)] for t in range(3)]
            rolled = [[pltpu.roll(here[t][m], 7, 0) for m in range(3)] for t in range(3)]

            def steps(t):
                rows = pl.ds(8 * t, 8)
                values, old, squares = [], [], None
                for m in range(3):
                    f = here[t][m]
                    along_z = (src[z + 1, m, rows, :] - f) * z_mask
                    along_y = jnp.where(sub == 7, rolled[(t + 1) % 3][m], rolled[t][m]) - f
                    if t:
                        along_y = along_y * y_mask[t]
                    along_x = (pltpu.roll(f, NX - 1, 1) - f) * x_mask
                    triple = [along_z, along_y, along_x]
                    if turn:
                        past = [dual[z, 3 * m + d, rows, :] for d in range(3)]
                        triple = [a + b for a, b in zip(triple, past)]
                        old.append(past)
                    values.append(triple)
                    for v in triple:
                        squares = v * v if squares is None else squares + v * v
                scale = threshold * lax.rsqrt(jnp.maximum(squares, limit))
                twice = scale + scale
                moved = []
                for m in range(3):
                    if turn < 2:
                        for d in range(3):
                            dual[z, 3 * m + d, rows, :] = values[m][d] * scale
                    triple = [v * twice for v in values[m]]
                    if turn:
                        triple = [a - b for a, b in zip(triple, old[m])]
                    moved.append(triple)
                return moved

            def inner(t, moved):
                rows = pl.ds(8 * t, 8)
                partial, turned = [], []
                for m in range(3):
                    step_z, step_y, step_x = moved[m]
                    total = step_z - carry[m, rows, :]
                    carry[m, rows, :] = step_z
                    total = total + (step_x - pltpu.roll(step_x, 1, 1)) + step_y
                    partial.append(total + 12.0 * here[t][m])
                    turned.append(pltpu.roll(step_y, 1, 0))
                return partial, turned

            def finish(t, partial, own, earlier):
                rows = pl.ds(8 * t, 8)
                total = [
                    partial[m] - jnp.where(sub == 0, earlier[m], own[m]) for m in range(3)
                ]
                for m in range(3):
                    value = (
                        base[z, m, rows, :]
                        + scaled[m][0] * total[0]
                        + scaled[m][1] * total[1]
                        + scaled[m][2] * total[2]
                    )
                    if turn < 2:
                        field[z, m, rows, :] = value
                    else:
                        result[z - 2, m, rows, :] = value

            moved = steps(2)
            if turn < 2:
                partial_two, turned_two = inner(2, moved)
            else:
                turned_two = [pltpu.roll(moved[m][1], 1, 0) for m in range(3)]
            partial, turned_zero = inner(0, steps(0))
            finish(0, partial, turned_zero, turned_two)
            partial, turned_one = inner(1, steps(1))
            finish(1, partial, turned_one, turned_zero)
            if turn < 2:
                finish(2, partial_two, turned_two, turned_one)
            return 0

        lax.fori_loop(turn, LAYERS - 1 - turn, body, 0)

    for turn in range(3):
        sweep(turn)

    def send(layer):
        return pltpu.make_async_remote_copy(
            src_ref=result.at[1 + layer],
            dst_ref=out.at[:, pl.ds(pl.multiple_of(yb * 16, 16), 16)],
            send_sem=out_send.at[layer],
            recv_sem=out_recv.at[yb],
            device_id=(xh * 2 + pz0, xl * 16 + layer),
            device_id_type=MESH,
        )

    own_layer = pz0 * 8 + xl * 4 + py

    def send_body(i, _):
        layer = (i + py) % 4 + 4 * ((i // 4) ^ (xl + 2 * pz0))
        mine = jnp.logical_and(home, layer == own_layer)

        @pl.when(mine)
        def _():
            pltpu.make_async_copy(
                result.at[1 + layer],
                out.at[:, pl.ds(pl.multiple_of(yb * 16, 16), 16)],
                out_recv.at[yb],
            ).start()

        @pl.when(jnp.logical_not(mine))
        def _():
            send(layer).start()

        return 0

    lax.fori_loop(0, 16, send_body, 0)

    def drain_swap(q, _):
        swap(q).wait_send()
        return 0

    lax.fori_loop(0, 8, drain_swap, 0)

    def drain_two(i, _):
        one(i).wait_send()
        two_sent(i, 0)
        two_sent(i, 1)
        return 0

    lax.fori_loop(0, PIECES, drain_two, 0)

    for which in range(2):
        @pl.when((has_below, has_above)[which])
        def _():
            halo_z(which).wait_send()

        @pl.when((has_before, has_after)[which])
        def _():
            halo_y(which, 0).wait_send()
            halo_y(which, 1).wait_send()

    def drain_out(i, _):
        @pl.when(jnp.logical_not(jnp.logical_and(home, i == own_layer)))
        def _():
            send(i).wait_send()

        pltpu.make_async_remote_copy(
            src_ref=result.at[0],
            dst_ref=out.at[:, pl.ds(pl.multiple_of(i * 16, 16), 16)],
            send_sem=out_send.at[0],
            recv_sem=out_recv.at[i],
            device_id=partner,
            device_id_type=MESH,
        ).wait_recv()
        return 0

    lax.fori_loop(0, 16, drain_out, 0)


def on_device(volumes, attenuation, penalty, tv_weight):
    vol = volumes.reshape(2, 4, 8, 2, 16, NX)
    dma = pltpu.SemaphoreType.DMA
    out = pl.pallas_call(
        kernel,
        out_shape=jax.ShapeDtypeStruct((3, 256, NX), F32),
        in_specs=[pl.BlockSpec(memory_space=pl.ANY)]
        + [pl.BlockSpec(memory_space=pltpu.SMEM)] * 3,
        out_specs=pl.BlockSpec(memory_space=pl.ANY),
        scratch_shapes=[
            pltpu.VMEM((4, 4, 8, 16, NX), F32),
            pltpu.VMEM((8, 4, 3, 16, NX), F32),
            pltpu.VMEM((4, 4, 3, 16, NX), F32),
            pltpu.VMEM((2, 4, 4, 3, 16, NX), F32),
            pltpu.VMEM((LAYERS, 3, 24, NX), F32),
            pltpu.VMEM((LAYERS, 3, 24, NX), F32),
            pltpu.VMEM((LAYERS, 9, 24, NX), F32),
            pltpu.VMEM((3, 24, NX), F32),
            pltpu.VMEM((11, 3, 8, NX), F32),
            pltpu.VMEM((11, 3, 8, NX), F32),
            pltpu.VMEM((11, 3, 8, NX), F32),
            pltpu.VMEM((11, 3, 8, NX), F32),
            pltpu.VMEM((17, 3, 16, NX), F32),
            dma((8,)), dma((8,)), dma((8,)),
            dma((PIECES,)), dma((PIECES,)),
            dma((2 * PIECES,)), dma((2 * PIECES,)),
            dma((2,)), dma((2,)), dma((4,)), dma((4,)),
            dma((16,)), dma((16,)),
        ],
        compiler_params=pltpu.CompilerParams(
            collective_id=0, has_side_effects=True, vmem_limit_bytes=56 * 1024 * 1024
        ),
        cost_estimate=pl.CostEstimate(
            flops=60_000_000, bytes_accessed=8_000_000, transcendentals=400_000
        ),
    )(vol, attenuation, penalty, tv_weight)
    return out.reshape(3, 1, 256, NX)


def solution(mesh):
    placed = (P("bin", "slab", None, None), P(), P(), P())
    return jax.shard_map(
        on_device,
        mesh=mesh,
        in_specs=placed,
        out_specs=P(None, ("bin", "slab"), None, None),
        check_vma=False,
    )
```

```python
import jax
import jax.numpy as jnp
from jax import lax
from jax.experimental import pallas as pl
from jax.experimental.pallas import tpu as pltpu
from jax.sharding import PartitionSpec as P

MESH = pl.DeviceIdType.MESH
F32 = jnp.float32
HALO = 3
LAYERS = 16 + 2 * HALO
NX = 512
LAG = 4
PIECES = 16


def position():
    bin_index = lax.axis_index("bin")
    slab_index = lax.axis_index("slab")
    return (
        bin_index // 2,
        bin_index % 2,
        slab_index // 16,
        (slab_index // 8) % 2,
        (slab_index // 4) % 2,
        slab_index % 4,
    )


def device(xh, core, pz1, pz0, xl, py):
    return (xh * 2 + core, pz1 * 16 + pz0 * 8 + xl * 4 + py)


def block_device(zb, yb):
    pz0 = (zb // 2) % 2
    return device(zb // 4, yb % 2, yb // 8, pz0, (zb % 2) ^ pz0, (yb // 2) % 4)


def scalars(att, penalty, tv_weight, xh):
    rho = penalty[0]
    threshold = tv_weight[0] / rho
    gram = [[None] * 3 for _ in range(3)]
    for i in range(3):
        for j in range(i, 3):
            total = att[i, 0] * att[j, 0]
            for k in range(1, 8):
                total = total + att[i, k] * att[j, k]
            gram[i][j] = gram[j][i] = total + 12.0 * rho if i == j else total
    cofactor = [
        [
            gram[(r + 1) % 3][(c + 1) % 3] * gram[(r + 2) % 3][(c + 2) % 3]
            - gram[(r + 1) % 3][(c + 2) % 3] * gram[(r + 2) % 3][(c + 1) % 3]
            for c in range(3)
        ]
        for r in range(3)
    ]
    determinant = sum(gram[0][c] * cofactor[0][c] for c in range(3))
    inverse = [[cofactor[c][r] / determinant for c in range(3)] for r in range(3)]
    weight = [
        [sum(inverse[m][n] * att[n, 4 * xh + k] for n in range(3)) for k in range(4)]
        for m in range(3)
    ]
    scaled = [[rho * inverse[m][n] for n in range(3)] for m in range(3)]
    return threshold, weight, scaled


def kernel(
    vol, att, penalty, tv_weight, out,
    raw, part, passed, landed, base, field_one, field_two, dual_zero, dual_one, carry,
    pack_lo, pack_hi, got_lo, got_hi, result,
    load_sem, core_send, core_recv, one_send, one_recv, two_send, two_recv,
    hz_send, hz_recv, hy_send, hy_recv, out_send, out_recv,
):
    xh, core, pz1, pz0, xl, py = position()
    turned_xl = xl ^ pz0
    zb = xh * 4 + pz0 * 2 + turned_xl
    yb = pz1 * 8 + py * 2 + core
    partner = device(xh, 1 - core, pz1, pz0, xl, py)
    across = device(xh, core, 1 - pz1, pz0, xl, py)

    def bins_at(n):
        return n // 2, pl.ds(((1 - n % 2) ^ pz1) * 4, 4)

    def load(n):
        layer, rows = bins_at(n)
        return pltpu.make_async_copy(
            vol.at[:, layer, rows, core], raw.at[pl.ds(core * 2, 2), layer, rows], load_sem.at[n]
        )

    def load_body(n, _):
        load(n).start()
        return 0

    lax.fori_loop(0, 8, load_body, 0)

    barrier = pltpu.get_barrier_semaphore()

    def greet(target):
        pl.semaphore_signal(barrier, inc=1, device_id=target, device_id_type=MESH)

    greet(partner)
    greet(across)
    for side in range(2):
        for row in range(4):
            target = device(side, core, pz1, pz0, turned_xl, row)

            @pl.when(jnp.logical_or(jnp.logical_or(side != xh, row != py), pz0 == 1))
            def _():
                greet(target)

    for dz in (1, 7):
        greet(block_device((zb + dz) % 8, yb))
    for dy in (1, 15):
        greet(block_device(zb, (yb + dy) % 16))

    home = jnp.logical_and(pz0 == core, pz1 == turned_xl)

    def greet_body(y, _):
        source = device(xh, y % 2, y // 8, core, pz1 ^ core, (y // 2) % 4)

        @pl.when(jnp.logical_not(jnp.logical_and(home, y == yb)))
        def _():
            greet(source)

        return 0

    lax.fori_loop(0, 16, greet_body, 0)

    threshold, weight, scaled = scalars(att, penalty, tv_weight, xh)

    @pl.when(zb == 0)
    def _():
        base[pl.ds(0, HALO)] = jnp.zeros((HALO, 3, 24, NX), F32)

    @pl.when(zb == 7)
    def _():
        base[pl.ds(16 + HALO, HALO)] = jnp.zeros((HALO, 3, 24, NX), F32)

    @pl.when(yb == 0)
    def _():
        got_lo[...] = jnp.zeros_like(got_lo)

    @pl.when(yb == 15)
    def _():
        got_hi[...] = jnp.zeros_like(got_hi)

    pl.semaphore_wait(barrier, 2 + 7 + pz0 + 4 + 16 - jnp.where(home, 1, 0))

    def swap(n):
        layer, rows = bins_at(n)
        return pltpu.make_async_remote_copy(
            src_ref=vol.at[:, layer, rows, 1 - core],
            dst_ref=raw.at[pl.ds(core * 2, 2), layer, rows],
            send_sem=core_send.at[n],
            recv_sem=core_recv.at[n],
            device_id=partner,
            device_id_type=MESH,
        )

    def swap_body(n, _):
        swap(n).start()
        return 0

    lax.fori_loop(0, 4, swap_body, 0)

    def project(n):
        load(n).wait()
        swap(n).wait_recv()

        @pl.when(n < 4)
        def _():
            swap(n + 4).start()

        layer = n // 2
        first = ((1 - n % 2) ^ pz1) * 4

        def body(k, _):
            q = first + k
            for r in range(2):
                rows = pl.ds(8 * r, 8)
                bins = [raw[b, layer, q, rows, :] for b in range(4)]
                for m in range(3):
                    part[q, layer, m, rows, :] = (
                        weight[m][0] * bins[0]
                        + weight[m][1] * bins[1]
                        + weight[m][2] * bins[2]
                        + weight[m][3] * bins[3]
                    )
            return 0

        lax.fori_loop(0, 4, body, 0)

    def ahead(i):
        k = i % 4
        return jnp.where(k < 2, 2 * k + 1, 6 - 2 * k)

    def piece(i):
        return (py + ahead(i)) % 4, i // 4

    def one(i):
        row, h = piece(i)
        return pltpu.make_async_remote_copy(
            src_ref=part.at[(1 - pz1) * 4 + row, h],
            dst_ref=passed.at[row, h],
            send_sem=one_send.at[i],
            recv_sem=one_recv.at[i],
            device_id=across,
            device_id_type=MESH,
        )

    def two(i, passing):
        row, h = piece(i)
        source = passed.at[row, h] if passing else part.at[pz1 * 4 + row, h]
        return pltpu.make_async_remote_copy(
            src_ref=source,
            dst_ref=landed.at[xh, py, h],
            send_sem=two_send.at[i + PIECES * passing],
            recv_sem=two_recv.at[(xh * 4 + py) * 4 + h],
            device_id=device(1 - pz1 if passing else pz1, core, pz1, pz0, turned_xl, row),
            device_id_type=MESH,
        )

    def two_stays(i, passing):
        same = jnp.logical_and(xh == (1 - pz1 if passing else pz1), ahead(i) == 0)
        return jnp.logical_and(same, pz0 == 0)

    def two_start(i, passing):
        row, h = piece(i)
        stays = two_stays(i, passing)
        source = passed.at[row, h] if passing else part.at[pz1 * 4 + row, h]

        @pl.when(stays)
        def _():
            pltpu.make_async_copy(
                source, landed.at[xh, py, h], two_recv.at[(xh * 4 + py) * 4 + h]
            ).start()

        @pl.when(jnp.logical_not(stays))
        def _():
            two(i, passing).start()

    def two_sent(i, passing):
        @pl.when(jnp.logical_not(two_stays(i, passing)))
        def _():
            two(i, passing).wait_send()

    def pass_on(i):
        one(i).wait_recv()
        two_start(i, 1)

    def input_body(i, _):
        @pl.when(i % 4 == 0)
        def _():
            project(i // 2)
            project(i // 2 + 1)

        one(i).start()
        two_start(i, 0)

        @pl.when(i >= LAG)
        def _():
            pass_on(i - LAG)

        return 0

    lax.fori_loop(0, PIECES, input_body, 0)

    def tail_body(i, _):
        pass_on(i)
        return 0

    lax.fori_loop(PIECES - LAG, PIECES, tail_body, 0)

    below = block_device((zb + 7) % 8, yb)
    above = block_device((zb + 1) % 8, yb)
    before = block_device(zb, (yb + 15) % 16)
    after = block_device(zb, (yb + 1) % 16)
    has_below, has_above = zb > 0, zb < 7
    has_before, has_after = yb > 0, yb < 15

    def halo_z(which, n):
        first, target, place = ((HALO, below, 16 + HALO), (16, above, 0))[which]
        return pltpu.make_async_remote_copy(
            src_ref=base.at[first + n, :, pl.ds(0, 16)],
            dst_ref=base.at[place + n, :, pl.ds(0, 16)],
            send_sem=hz_send.at[which * 3 + n],
            recv_sem=hz_recv.at[which * 3 + n],
            device_id=target,
            device_id_type=MESH,
        )

    def halo_y(which, n):
        pack, got, target = ((pack_lo, got_hi, before), (pack_hi, got_lo, after))[which]
        late = isinstance(n, int) and n == 4
        rows = pl.ds(8, 3) if late else pl.ds(2 * n, 2)
        return pltpu.make_async_remote_copy(
            src_ref=pack.at[rows],
            dst_ref=got.at[rows],
            send_sem=hy_send.at[which * 5 + n],
            recv_sem=hy_recv.at[which * 5 + n],
            device_id=target,
            device_id_type=MESH,
        )

    sub = lax.broadcasted_iota(jnp.int32, (8, NX), 0)

    def pair(at, late):
        if late:
            return at - 8, at + 11
        first = HALO + at // 2 + 4 * (at % 2)
        return first, first + 8

    def pack_pair(at, late):
        first, second = pair(at, late)
        for m in range(3):
            lo_first = base[first, m, pl.ds(0, 8), :]
            lo_second = pltpu.roll(base[second, m, pl.ds(0, 8), :], 4, 0)
            pack_lo[at, m] = jnp.where(sub < 4, lo_first, lo_second)
            hi_first = base[first, m, pl.ds(8, 8), :]
            hi_second = pltpu.roll(base[second, m, pl.ds(8, 8), :], 4, 0)
            pack_hi[at, m] = jnp.where(sub < 4, hi_second, hi_first)

    def unpack_pair(at, late):
        first, second = pair(at, late)
        for m in range(3):
            lo = got_lo[at, m]
            hi = got_hi[at, m]
            base[first, m, pl.ds(16, 8), :] = jnp.where(sub < 4, hi, lo)
            base[second, m, pl.ds(16, 8), :] = pltpu.roll(jnp.where(sub < 4, lo, hi), 4, 0)

    def reduce_body(h, _):
        def piece_body(k, _):
            row = (py + 4 - ahead(k)) % 4
            for side in range(2):
                pltpu.make_async_remote_copy(
                    src_ref=landed.at[side, row, h],
                    dst_ref=landed.at[side, row, h],
                    send_sem=two_send.at[0],
                    recv_sem=two_recv.at[(side * 4 + row) * 4 + h],
                    device_id=partner,
                    device_id_type=MESH,
                ).wait_recv()
            layer = HALO + row * 4 + h
            for m in range(3):
                base[layer, m, pl.ds(0, 16), :] = landed[0, row, h, m] + landed[1, row, h, m]
            return 0

        lax.fori_loop(0, 4, piece_body, 0)

        @pl.when(jnp.logical_and(has_below, h < 3))
        def _():
            halo_z(0, h).start()

        @pl.when(jnp.logical_and(has_above, h > 0))
        def _():
            halo_z(1, h - 1).start()

        for half in range(2):
            pack_pair(2 * h + half, False)

        @pl.when(has_before)
        def _():
            halo_y(0, h).start()

        @pl.when(has_after)
        def _():
            halo_y(1, h).start()

        return 0

    lax.fori_loop(0, 4, reduce_body, 0)

    def arrive_y(n):
        @pl.when(has_after)
        def _():
            halo_y(0, n).wait_recv()

        @pl.when(has_before)
        def _():
            halo_y(1, n).wait_recv()

    def arrive_body(h, _):
        arrive_y(h)
        for half in range(2):
            unpack_pair(2 * h + half, False)
        return 0

    lax.fori_loop(0, 4, arrive_body, 0)

    lane = lax.broadcasted_iota(jnp.int32, (8, NX), 1)
    x_mask = jnp.where(lane == NX - 1, 0.0, 1.0).astype(F32)
    y_mask = {
        1: jnp.where(jnp.logical_and(sub == 7, yb == 15), 0.0, 1.0).astype(F32),
        2: jnp.where(jnp.logical_and(sub == 7, yb == 0), 0.0, 1.0).astype(F32),
    }
    limit = threshold * threshold

    def sweep(turn, first, last):
        src = (base, field_one, field_two)[turn]
        target = (field_one, field_two, result)[turn]
        dual = (dual_zero, dual_one, None)[turn]
        dual_past = (None, dual_zero, dual_one)[turn]

        def body(z, _):
            z_global = zb * 16 + z - HALO
            z_mask = jnp.where(
                jnp.logical_or(z_global == 127, z_global == -1), 0.0, 1.0
            ).astype(F32)
            here = [[src[z, m, pl.ds(8 * t, 8), :] for m in range(3)] for t in range(3)]
            rolled = [[pltpu.roll(here[t][m], 7, 0) for m in range(3)] for t in range(3)]

            def steps(t):
                rows = pl.ds(8 * t, 8)
                values, old, squares = [], [], None
                for m in range(3):
                    f = here[t][m]
                    along_z = (src[z + 1, m, rows, :] - f) * z_mask
                    along_y = jnp.where(sub == 7, rolled[(t + 1) % 3][m], rolled[t][m]) - f
                    if t:
                        along_y = along_y * y_mask[t]
                    along_x = (pltpu.roll(f, NX - 1, 1) - f) * x_mask
                    triple = [along_z, along_y, along_x]
                    if turn:
                        past = [dual_past[z, 3 * m + d, rows, :] for d in range(3)]
                        triple = [a + b for a, b in zip(triple, past)]
                        old.append(past)
                    values.append(triple)
                    for v in triple:
                        squares = v * v if squares is None else squares + v * v
                scale = threshold * lax.rsqrt(jnp.maximum(squares, limit))
                twice = scale + scale
                moved = []
                for m in range(3):
                    if turn < 2:
                        for d in range(3):
                            dual[z, 3 * m + d, rows, :] = values[m][d] * scale
                    triple = [v * twice for v in values[m]]
                    if turn:
                        triple = [a - b for a, b in zip(triple, old[m])]
                    moved.append(triple)
                return moved

            def inner(t, moved):
                rows = pl.ds(8 * t, 8)
                partial, turned = [], []
                for m in range(3):
                    step_z, step_y, step_x = moved[m]
                    total = step_z - carry[turn, m, rows, :]
                    carry[turn, m, rows, :] = step_z
                    total = total + (step_x - pltpu.roll(step_x, 1, 1)) + step_y
                    partial.append(total + 12.0 * here[t][m])
                    turned.append(pltpu.roll(step_y, 1, 0))
                return partial, turned

            def finish(t, partial, own, earlier):
                rows = pl.ds(8 * t, 8)
                total = [
                    partial[m] - jnp.where(sub == 0, earlier[m], own[m]) for m in range(3)
                ]
                for m in range(3):
                    value = (
                        base[z, m, rows, :]
                        + scaled[m][0] * total[0]
                        + scaled[m][1] * total[1]
                        + scaled[m][2] * total[2]
                    )
                    target[z - 2 if turn == 2 else z, m, rows, :] = value

            moved = steps(2)
            if turn < 2:
                partial_two, turned_two = inner(2, moved)
            else:
                turned_two = [pltpu.roll(moved[m][1], 1, 0) for m in range(3)]
            partial, turned_zero = inner(0, steps(0))
            finish(0, partial, turned_zero, turned_two)
            partial, turned_one = inner(1, steps(1))
            finish(1, partial, turned_one, turned_zero)
            if turn < 2:
                finish(2, partial_two, turned_two, turned_one)
            return 0

        lax.fori_loop(first, last + 1, body, 0)

    def send(layer):
        return pltpu.make_async_remote_copy(
            src_ref=result.at[1 + layer],
            dst_ref=out.at[:, pl.ds(pl.multiple_of(yb * 16, 16), 16)],
            send_sem=out_send.at[layer],
            recv_sem=out_recv.at[yb],
            device_id=(xh * 2 + pz0, turned_xl * 16 + layer),
            device_id_type=MESH,
        )

    own_layer = pz0 * 8 + xl * 4 + py

    def send_layer(layer):
        mine = jnp.logical_and(home, layer == own_layer)

        @pl.when(mine)
        def _():
            pltpu.make_async_copy(
                result.at[1 + layer],
                out.at[:, pl.ds(pl.multiple_of(yb * 16, 16), 16)],
                out_recv.at[yb],
            ).start()

        @pl.when(jnp.logical_not(mine))
        def _():
            send(layer).start()

    spread = py + 4 * (xl + 2 * pz0)

    def send_inner(i, _):
        send_layer(3 + (i + spread) % 10)
        return 0

    def send_outer(i, _):
        k = (i + spread) % 6
        send_layer(jnp.where(k < 3, k, k + 10))
        return 0

    sweep(0, 3, 17)
    for n in range(3):
        @pl.when(has_above)
        def _():
            halo_z(0, n).wait_recv()

        @pl.when(has_below)
        def _():
            halo_z(1, n).wait_recv()

    for at in range(8, 11):
        pack_pair(at, True)

    @pl.when(has_before)
    def _():
        halo_y(0, 4).start()

    @pl.when(has_after)
    def _():
        halo_y(1, 4).start()

    sweep(1, 4, 16)
    sweep(2, 5, 15)
    lax.fori_loop(0, 10, send_inner, 0)
    arrive_y(4)
    for at in range(8, 11):
        unpack_pair(at, True)
    sweep(0, 18, 20)
    sweep(0, 0, 3)
    sweep(1, 17, 19)
    sweep(1, 1, 4)
    sweep(2, 16, 18)
    sweep(2, 2, 5)
    lax.fori_loop(0, 6, send_outer, 0)

    def drain_swap(q, _):
        swap(q).wait_send()
        return 0

    lax.fori_loop(0, 8, drain_swap, 0)

    def drain_two(i, _):
        one(i).wait_send()
        two_sent(i, 0)
        two_sent(i, 1)
        return 0

    lax.fori_loop(0, PIECES, drain_two, 0)

    for which in range(2):
        @pl.when((has_below, has_above)[which])
        def _():
            for n in range(3):
                halo_z(which, n).wait_send()

        @pl.when((has_before, has_after)[which])
        def _():
            for n in range(5):
                halo_y(which, n).wait_send()

    def drain_out(i, _):
        @pl.when(jnp.logical_not(jnp.logical_and(home, i == own_layer)))
        def _():
            send(i).wait_send()

        pltpu.make_async_remote_copy(
            src_ref=result.at[0],
            dst_ref=out.at[:, pl.ds(pl.multiple_of(i * 16, 16), 16)],
            send_sem=out_send.at[0],
            recv_sem=out_recv.at[i],
            device_id=partner,
            device_id_type=MESH,
        ).wait_recv()
        return 0

    lax.fori_loop(0, 16, drain_out, 0)


def on_device(volumes, attenuation, penalty, tv_weight):
    vol = volumes.reshape(2, 4, 8, 2, 16, NX)
    dma = pltpu.SemaphoreType.DMA
    out = pl.pallas_call(
        kernel,
        out_shape=jax.ShapeDtypeStruct((3, 256, NX), F32),
        in_specs=[pl.BlockSpec(memory_space=pl.ANY)]
        + [pl.BlockSpec(memory_space=pltpu.SMEM)] * 3,
        out_specs=pl.BlockSpec(memory_space=pl.ANY),
        scratch_shapes=[
            pltpu.VMEM((4, 4, 8, 16, NX), F32),
            pltpu.VMEM((8, 4, 3, 16, NX), F32),
            pltpu.VMEM((4, 4, 3, 16, NX), F32),
            pltpu.VMEM((2, 4, 4, 3, 16, NX), F32),
            pltpu.VMEM((LAYERS, 3, 24, NX), F32),
            pltpu.VMEM((LAYERS, 3, 24, NX), F32),
            pltpu.VMEM((LAYERS, 3, 24, NX), F32),
            pltpu.VMEM((LAYERS, 9, 24, NX), F32),
            pltpu.VMEM((LAYERS, 9, 24, NX), F32),
            pltpu.VMEM((3, 3, 24, NX), F32),
            pltpu.VMEM((11, 3, 8, NX), F32),
            pltpu.VMEM((11, 3, 8, NX), F32),
            pltpu.VMEM((11, 3, 8, NX), F32),
            pltpu.VMEM((11, 3, 8, NX), F32),
            pltpu.VMEM((17, 3, 16, NX), F32),
            dma((8,)), dma((8,)), dma((8,)),
            dma((PIECES,)), dma((PIECES,)),
            dma((2 * PIECES,)), dma((2 * PIECES,)),
            dma((6,)), dma((6,)), dma((10,)), dma((10,)),
            dma((16,)), dma((16,)),
        ],
        compiler_params=pltpu.CompilerParams(
            collective_id=0, has_side_effects=True, vmem_limit_bytes=51 * 1024 * 1024
        ),
        cost_estimate=pl.CostEstimate(
            flops=60_000_000, bytes_accessed=8_000_000, transcendentals=400_000
        ),
    )(vol, attenuation.T, penalty, tv_weight)
    return out.reshape(3, 1, 256, NX)


def solution(mesh):
    placed = (P("bin", "slab", None, None), P(), P(), P())
    return jax.shard_map(
        on_device,
        mesh=mesh,
        in_specs=placed,
        out_specs=P(None, ("bin", "slab"), None, None),
        check_vma=False,
    )
```

```python
import jax
import jax.numpy as jnp
from jax import lax
from jax.experimental import pallas as pl
from jax.experimental.pallas import tpu as pltpu
from jax.sharding import PartitionSpec as P

MESH = pl.DeviceIdType.MESH
F32 = jnp.float32
HALO = 3
LAYERS = 16 + 2 * HALO
NX = 512
LAG = 4
PIECES = 16


def position():
    bin_index = lax.axis_index("bin")
    slab_index = lax.axis_index("slab")
    return (
        bin_index // 2,
        bin_index % 2,
        slab_index // 16,
        (slab_index // 8) % 2,
        (slab_index // 4) % 2,
        slab_index % 4,
    )


def device(xh, core, pz1, pz0, xl, py):
    return (xh * 2 + core, pz1 * 16 + pz0 * 8 + xl * 4 + py)


def block_device(zb, yb):
    pz0 = (zb // 2) % 2
    return device(zb // 4, yb % 2, yb // 8, pz0, (zb % 2) ^ pz0, (yb // 2) % 4)


def scalars(att, penalty, tv_weight, xh):
    rho = penalty[0]
    threshold = tv_weight[0] / rho
    gram = [[None] * 3 for _ in range(3)]
    for i in range(3):
        for j in range(i, 3):
            total = att[i, 0] * att[j, 0]
            for k in range(1, 8):
                total = total + att[i, k] * att[j, k]
            gram[i][j] = gram[j][i] = total + 12.0 * rho if i == j else total
    cofactor = [
        [
            gram[(r + 1) % 3][(c + 1) % 3] * gram[(r + 2) % 3][(c + 2) % 3]
            - gram[(r + 1) % 3][(c + 2) % 3] * gram[(r + 2) % 3][(c + 1) % 3]
            for c in range(3)
        ]
        for r in range(3)
    ]
    determinant = sum(gram[0][c] * cofactor[0][c] for c in range(3))
    inverse = [[cofactor[c][r] / determinant for c in range(3)] for r in range(3)]
    weight = [
        [sum(inverse[m][n] * att[n, 4 * xh + k] for n in range(3)) for k in range(4)]
        for m in range(3)
    ]
    scaled = [[rho * inverse[m][n] for n in range(3)] for m in range(3)]
    return threshold, weight, scaled


def kernel(
    vol, att, penalty, tv_weight, out,
    raw, part, passed, landed, base, field_one, field_two, dual_zero, dual_one, div_zero, div_one, carry,
    pack_lo, pack_hi, got_lo, got_hi, result,
    load_sem, core_send, core_recv, one_send, one_recv, two_send, two_recv,
    hz_send, hz_recv, hy_send, hy_recv, out_send, out_recv,
):
    xh, core, pz1, pz0, xl, py = position()
    turned_xl = xl ^ pz0
    zb = xh * 4 + pz0 * 2 + turned_xl
    yb = pz1 * 8 + py * 2 + core
    partner = device(xh, 1 - core, pz1, pz0, xl, py)
    across = device(xh, core, 1 - pz1, pz0, xl, py)

    def bins_at(n):
        return n // 2, pl.ds(((1 - n % 2) ^ pz1) * 4, 4)

    def load(n):
        layer, rows = bins_at(n)
        return pltpu.make_async_copy(
            vol.at[:, layer, rows, core], raw.at[pl.ds(core * 2, 2), layer, rows], load_sem.at[n]
        )

    def load_body(n, _):
        load(n).start()
        return 0

    lax.fori_loop(0, 8, load_body, 0)

    barrier = pltpu.get_barrier_semaphore()

    def greet(target):
        pl.semaphore_signal(barrier, inc=1, device_id=target, device_id_type=MESH)

    greet(partner)
    greet(across)
    for side in range(2):
        for row in range(4):
            target = device(side, core, pz1, pz0, turned_xl, row)

            @pl.when(jnp.logical_or(jnp.logical_or(side != xh, row != py), pz0 == 1))
            def _():
                greet(target)

    for dz in (1, 7):
        greet(block_device((zb + dz) % 8, yb))
    for dy in (1, 15):
        greet(block_device(zb, (yb + dy) % 16))

    home = jnp.logical_and(pz0 == core, pz1 == turned_xl)

    def greet_body(y, _):
        source = device(xh, y % 2, y // 8, core, pz1 ^ core, (y // 2) % 4)

        @pl.when(jnp.logical_not(jnp.logical_and(home, y == yb)))
        def _():
            greet(source)

        return 0

    lax.fori_loop(0, 16, greet_body, 0)

    threshold, weight, scaled = scalars(att, penalty, tv_weight, xh)

    @pl.when(zb == 0)
    def _():
        base[pl.ds(0, HALO)] = jnp.zeros((HALO, 3, 24, NX), F32)

    @pl.when(zb == 7)
    def _():
        base[pl.ds(16 + HALO, HALO)] = jnp.zeros((HALO, 3, 24, NX), F32)

    @pl.when(yb == 0)
    def _():
        got_lo[...] = jnp.zeros_like(got_lo)

    @pl.when(yb == 15)
    def _():
        got_hi[...] = jnp.zeros_like(got_hi)

    pl.semaphore_wait(barrier, 2 + 7 + pz0 + 4 + 16 - jnp.where(home, 1, 0))

    def swap(n):
        layer, rows = bins_at(n)
        return pltpu.make_async_remote_copy(
            src_ref=vol.at[:, layer, rows, 1 - core],
            dst_ref=raw.at[pl.ds(core * 2, 2), layer, rows],
            send_sem=core_send.at[n],
            recv_sem=core_recv.at[n],
            device_id=partner,
            device_id_type=MESH,
        )

    def swap_body(n, _):
        swap(n).start()
        return 0

    lax.fori_loop(0, 4, swap_body, 0)

    def project(n):
        load(n).wait()
        swap(n).wait_recv()

        @pl.when(n < 4)
        def _():
            swap(n + 4).start()

        layer = n // 2
        first = ((1 - n % 2) ^ pz1) * 4

        def body(k, _):
            q = first + k
            for r in range(2):
                rows = pl.ds(8 * r, 8)
                bins = [raw[b, layer, q, rows, :] for b in range(4)]
                for m in range(3):
                    part[q, layer, m, rows, :] = (
                        weight[m][0] * bins[0]
                        + weight[m][1] * bins[1]
                        + weight[m][2] * bins[2]
                        + weight[m][3] * bins[3]
                    )
            return 0

        lax.fori_loop(0, 4, body, 0)

    def ahead(i):
        k = i % 4
        return (jnp.where(k < 2, 2 * k + 1, 6 - 2 * k) + 2 * core) % 4

    def piece(i):
        return (py + ahead(i)) % 4, i // 4

    def one(i):
        row, h = piece(i)
        return pltpu.make_async_remote_copy(
            src_ref=part.at[(1 - pz1) * 4 + row, h],
            dst_ref=passed.at[row, h],
            send_sem=one_send.at[i],
            recv_sem=one_recv.at[i],
            device_id=across,
            device_id_type=MESH,
        )

    def two(i, passing):
        row, h = piece(i)
        source = passed.at[row, h] if passing else part.at[pz1 * 4 + row, h]
        return pltpu.make_async_remote_copy(
            src_ref=source,
            dst_ref=landed.at[xh, py, h],
            send_sem=two_send.at[i + PIECES * passing],
            recv_sem=two_recv.at[(xh * 4 + py) * 4 + h],
            device_id=device(1 - pz1 if passing else pz1, core, pz1, pz0, turned_xl, row),
            device_id_type=MESH,
        )

    def two_stays(i, passing):
        same = jnp.logical_and(xh == (1 - pz1 if passing else pz1), ahead(i) == 0)
        return jnp.logical_and(same, pz0 == 0)

    def two_start(i, passing):
        row, h = piece(i)
        stays = two_stays(i, passing)
        source = passed.at[row, h] if passing else part.at[pz1 * 4 + row, h]

        @pl.when(stays)
        def _():
            pltpu.make_async_copy(
                source, landed.at[xh, py, h], two_recv.at[(xh * 4 + py) * 4 + h]
            ).start()

        @pl.when(jnp.logical_not(stays))
        def _():
            two(i, passing).start()

    def two_sent(i, passing):
        @pl.when(jnp.logical_not(two_stays(i, passing)))
        def _():
            two(i, passing).wait_send()

    def pass_on(i):
        one(i).wait_recv()
        two_start(i, 1)

    def input_body(i, _):
        @pl.when(i % 4 == 0)
        def _():
            project(i // 2)
            project(i // 2 + 1)

        one(i).start()
        two_start(i, 0)

        @pl.when(i >= LAG)
        def _():
            pass_on(i - LAG)

        return 0

    lax.fori_loop(0, PIECES, input_body, 0)

    def tail_body(i, _):
        pass_on(i)
        return 0

    lax.fori_loop(PIECES - LAG, PIECES, tail_body, 0)

    below = block_device((zb + 7) % 8, yb)
    above = block_device((zb + 1) % 8, yb)
    before = block_device(zb, (yb + 15) % 16)
    after = block_device(zb, (yb + 1) % 16)
    has_below, has_above = zb > 0, zb < 7
    has_before, has_after = yb > 0, yb < 15

    def halo_z(which, n):
        first, target, place = ((HALO, below, 16 + HALO), (16, above, 0))[which]
        return pltpu.make_async_remote_copy(
            src_ref=base.at[first + n, :, pl.ds(0, 16)],
            dst_ref=base.at[place + n, :, pl.ds(0, 16)],
            send_sem=hz_send.at[which * 3 + n],
            recv_sem=hz_recv.at[which * 3 + n],
            device_id=target,
            device_id_type=MESH,
        )

    def halo_y(which, n):
        pack, got, target = ((pack_lo, got_hi, before), (pack_hi, got_lo, after))[which]
        late = isinstance(n, int) and n == 4
        rows = pl.ds(8, 3) if late else pl.ds(2 * n, 2)
        return pltpu.make_async_remote_copy(
            src_ref=pack.at[rows],
            dst_ref=got.at[rows],
            send_sem=hy_send.at[which * 5 + n],
            recv_sem=hy_recv.at[which * 5 + n],
            device_id=target,
            device_id_type=MESH,
        )

    sub = lax.broadcasted_iota(jnp.int32, (8, NX), 0)

    def pair(at, late):
        if late:
            return at - 8, at + 11
        first = HALO + at // 2 + 4 * (at % 2)
        return first, first + 8

    def pack_pair(at, late):
        first, second = pair(at, late)
        for m in range(3):
            lo_first = base[first, m, pl.ds(0, 8), :]
            lo_second = pltpu.roll(base[second, m, pl.ds(0, 8), :], 4, 0)
            pack_lo[at, m] = jnp.where(sub < 4, lo_first, lo_second)
            hi_first = base[first, m, pl.ds(8, 8), :]
            hi_second = pltpu.roll(base[second, m, pl.ds(8, 8), :], 4, 0)
            pack_hi[at, m] = jnp.where(sub < 4, hi_second, hi_first)

    def unpack_pair(at, late):
        first, second = pair(at, late)
        for m in range(3):
            lo = got_lo[at, m]
            hi = got_hi[at, m]
            base[first, m, pl.ds(16, 8), :] = jnp.where(sub < 4, hi, lo)
            base[second, m, pl.ds(16, 8), :] = pltpu.roll(jnp.where(sub < 4, lo, hi), 4, 0)

    def reduce_body(h, _):
        def piece_body(k, _):
            row = (py + 4 - ahead(k)) % 4
            for side in range(2):
                pltpu.make_async_remote_copy(
                    src_ref=landed.at[side, row, h],
                    dst_ref=landed.at[side, row, h],
                    send_sem=two_send.at[0],
                    recv_sem=two_recv.at[(side * 4 + row) * 4 + h],
                    device_id=partner,
                    device_id_type=MESH,
                ).wait_recv()
            layer = HALO + row * 4 + h
            for m in range(3):
                base[layer, m, pl.ds(0, 16), :] = landed[0, row, h, m] + landed[1, row, h, m]
            return 0

        lax.fori_loop(0, 4, piece_body, 0)

        @pl.when(jnp.logical_and(has_below, h < 3))
        def _():
            halo_z(0, h).start()

        @pl.when(jnp.logical_and(has_above, h > 0))
        def _():
            halo_z(1, h - 1).start()

        for half in range(2):
            pack_pair(2 * h + half, False)

        @pl.when(has_before)
        def _():
            halo_y(0, h).start()

        @pl.when(has_after)
        def _():
            halo_y(1, h).start()

        return 0

    lax.fori_loop(0, 4, reduce_body, 0)

    def arrive_y(n):
        @pl.when(has_after)
        def _():
            halo_y(0, n).wait_recv()

        @pl.when(has_before)
        def _():
            halo_y(1, n).wait_recv()

    def arrive_body(h, _):
        arrive_y(h)
        for half in range(2):
            unpack_pair(2 * h + half, False)
        return 0

    lax.fori_loop(0, 4, arrive_body, 0)

    lane = lax.broadcasted_iota(jnp.int32, (8, 128), 1)
    y_mask = {
        1: jnp.where(jnp.logical_and(sub == 7, yb == 15), 0.0, 1.0).astype(F32),
        2: jnp.where(jnp.logical_and(sub == 7, yb == 0), 0.0, 1.0).astype(F32),
    }
    limit = threshold * threshold

    def next_x(f):
        parts = [f[:, k : k + 128] for k in range(0, f.shape[1], 128)]
        turned = [pltpu.roll(p, 127, 1) for p in parts]
        later = turned[1:] + parts[-1:]
        return jnp.concatenate(
            [jnp.where(lane == 127, b, a) for a, b in zip(turned, later)], axis=1
        )

    def last_x(p):
        parts = [p[:, k : k + 128] for k in range(0, p.shape[1], 128)]
        turned = [pltpu.roll(q, 1, 1) for q in parts]
        earlier = [jnp.zeros_like(parts[0])] + turned[:-1]
        return jnp.concatenate(
            [jnp.where(lane == 0, b, a) for a, b in zip(turned, earlier)], axis=1
        )

    def sweep(turn, first, last):
        src = (base, field_one, field_two)[turn]
        target = (field_one, field_two, result)[turn]
        dual = (dual_zero, dual_one, None)[turn]
        div = (div_zero, div_one, None)[turn]
        dual_past = (None, dual_zero, dual_one)[turn]
        div_past = (None, div_zero, div_one)[turn]

        def body(z, _):
            z_global = zb * 16 + z - HALO
            edge = jnp.logical_or(z_global == 127, z_global == -1)
            upper = z + jnp.where(edge, 0, 1)
            here = [[src[z, m, pl.ds(8 * t, 8), :] for m in range(3)] for t in range(3)]
            rolled = [[pltpu.roll(here[t][m], 7, 0) for m in range(3)] for t in range(3)]

            def duals(t):
                rows = pl.ds(8 * t, 8)
                values, squares = [], None
                for m in range(3):
                    f = here[t][m]
                    along_z = src[upper, m, rows, :] - f
                    along_y = jnp.where(sub == 7, rolled[(t + 1) % 3][m], rolled[t][m]) - f
                    if t:
                        along_y = along_y * y_mask[t]
                    along_x = next_x(f) - f
                    triple = [along_z, along_y, along_x]
                    if turn:
                        triple = [
                            triple[d] + dual_past[z, 3 * m + d, rows, :] for d in range(3)
                        ]
                    values.append(triple)
                    for v in triple:
                        squares = v * v if squares is None else squares + v * v
                scale = threshold * lax.rsqrt(jnp.maximum(squares, limit))
                fresh = [[v * scale for v in triple] for triple in values]
                if turn < 2:
                    for m in range(3):
                        for d in range(3):
                            dual[z, 3 * m + d, rows, :] = fresh[m][d]
                return fresh

            def inner(t, fresh):
                rows = pl.ds(8 * t, 8)
                partial, turned = [], []
                for m in range(3):
                    part_z, part_y, part_x = fresh[m]
                    total = part_z - carry[turn, m, rows, :]
                    carry[turn, m, rows, :] = part_z
                    partial.append(total + (part_x - last_x(part_x)) + part_y)
                    turned.append(pltpu.roll(part_y, 1, 0))
                return partial, turned

            def finish(t, partial, own, earlier):
                rows = pl.ds(8 * t, 8)
                total = []
                for m in range(3):
                    fresh_div = partial[m] - jnp.where(sub == 0, earlier[m], own[m])
                    if turn < 2:
                        div[z, m, rows, :] = fresh_div
                    step_div = fresh_div + fresh_div
                    if turn:
                        step_div = step_div - div_past[z, m, rows, :]
                    total.append(step_div + 12.0 * here[t][m])
                for m in range(3):
                    value = (
                        base[z, m, rows, :]
                        + scaled[m][0] * total[0]
                        + scaled[m][1] * total[1]
                        + scaled[m][2] * total[2]
                    )
                    target[z - 2 if turn == 2 else z, m, rows, :] = value

            fresh = duals(2)
            if turn < 2:
                partial_two, turned_two = inner(2, fresh)
            else:
                turned_two = [pltpu.roll(fresh[m][1], 1, 0) for m in range(3)]
            partial, turned_zero = inner(0, duals(0))
            finish(0, partial, turned_zero, turned_two)
            partial, turned_one = inner(1, duals(1))
            finish(1, partial, turned_one, turned_zero)
            if turn < 2:
                finish(2, partial_two, turned_two, turned_one)
            return 0

        lax.fori_loop(first, last + 1, body, 0)

    def send(layer):
        return pltpu.make_async_remote_copy(
            src_ref=result.at[1 + layer],
            dst_ref=out.at[:, pl.ds(pl.multiple_of(yb * 16, 16), 16)],
            send_sem=out_send.at[layer],
            recv_sem=out_recv.at[yb],
            device_id=(xh * 2 + pz0, turned_xl * 16 + layer),
            device_id_type=MESH,
        )

    own_layer = pz0 * 8 + xl * 4 + py

    def send_layer(layer):
        mine = jnp.logical_and(home, layer == own_layer)

        @pl.when(mine)
        def _():
            pltpu.make_async_copy(
                result.at[1 + layer],
                out.at[:, pl.ds(pl.multiple_of(yb * 16, 16), 16)],
                out_recv.at[yb],
            ).start()

        @pl.when(jnp.logical_not(mine))
        def _():
            send(layer).start()


    def layer_at(i):
        a, b = i % 4, i // 4
        low = (py + jnp.where(a < 2, 2 * a + 1, 6 - 2 * a) + 2 * core) % 4
        bit = xl ^ 1 ^ core ^ (b % 2)
        return low + 4 * bit + 8 * ((b // 2) ^ (a // 2) ^ pz1)

    def send_inner(i, _):
        layer = layer_at(i)

        @pl.when(jnp.logical_and(layer >= 3, layer <= 12))
        def _():
            send_layer(layer)

        return 0

    def send_outer(i, _):
        layer = layer_at(i)

        @pl.when(jnp.logical_or(layer < 3, layer > 12))
        def _():
            send_layer(layer)

        return 0

    sweep(0, 3, 17)
    for n in range(3):
        @pl.when(has_above)
        def _():
            halo_z(0, n).wait_recv()

        @pl.when(has_below)
        def _():
            halo_z(1, n).wait_recv()

    for at in range(8, 11):
        pack_pair(at, True)

    @pl.when(has_before)
    def _():
        halo_y(0, 4).start()

    @pl.when(has_after)
    def _():
        halo_y(1, 4).start()

    sweep(1, 4, 16)
    sweep(2, 5, 15)
    lax.fori_loop(0, 16, send_inner, 0)
    arrive_y(4)
    for at in range(8, 11):
        unpack_pair(at, True)
    sweep(0, 18, 20)
    sweep(0, 0, 3)
    sweep(1, 17, 19)
    sweep(1, 1, 4)
    sweep(2, 16, 18)
    sweep(2, 2, 5)
    lax.fori_loop(0, 16, send_outer, 0)

    def drain_swap(q, _):
        swap(q).wait_send()
        return 0

    lax.fori_loop(0, 8, drain_swap, 0)

    def drain_two(i, _):
        one(i).wait_send()
        two_sent(i, 0)
        two_sent(i, 1)
        return 0

    lax.fori_loop(0, PIECES, drain_two, 0)

    for which in range(2):
        @pl.when((has_below, has_above)[which])
        def _():
            for n in range(3):
                halo_z(which, n).wait_send()

        @pl.when((has_before, has_after)[which])
        def _():
            for n in range(5):
                halo_y(which, n).wait_send()

    def drain_out(i, _):
        @pl.when(jnp.logical_not(jnp.logical_and(home, i == own_layer)))
        def _():
            send(i).wait_send()

        pltpu.make_async_remote_copy(
            src_ref=result.at[0],
            dst_ref=out.at[:, pl.ds(pl.multiple_of(i * 16, 16), 16)],
            send_sem=out_send.at[0],
            recv_sem=out_recv.at[i],
            device_id=partner,
            device_id_type=MESH,
        ).wait_recv()
        return 0

    lax.fori_loop(0, 16, drain_out, 0)


def on_device(volumes, attenuation, penalty, tv_weight):
    vol = volumes.reshape(2, 4, 8, 2, 16, NX)
    dma = pltpu.SemaphoreType.DMA
    out = pl.pallas_call(
        kernel,
        out_shape=jax.ShapeDtypeStruct((3, 256, NX), F32),
        in_specs=[pl.BlockSpec(memory_space=pl.ANY)]
        + [pl.BlockSpec(memory_space=pltpu.SMEM)] * 3,
        out_specs=pl.BlockSpec(memory_space=pl.ANY),
        scratch_shapes=[
            pltpu.VMEM((4, 4, 8, 16, NX), F32),
            pltpu.VMEM((8, 4, 3, 16, NX), F32),
            pltpu.VMEM((4, 4, 3, 16, NX), F32),
            pltpu.VMEM((2, 4, 4, 3, 16, NX), F32),
            pltpu.VMEM((LAYERS, 3, 24, NX), F32),
            pltpu.VMEM((LAYERS, 3, 24, NX), F32),
            pltpu.VMEM((LAYERS, 3, 24, NX), F32),
            pltpu.VMEM((LAYERS, 9, 24, NX), F32),
            pltpu.VMEM((LAYERS, 9, 24, NX), F32),
            pltpu.VMEM((LAYERS, 3, 24, NX), F32),
            pltpu.VMEM((LAYERS, 3, 24, NX), F32),
            pltpu.VMEM((3, 3, 24, NX), F32),
            pltpu.VMEM((11, 3, 8, NX), F32),
            pltpu.VMEM((11, 3, 8, NX), F32),
            pltpu.VMEM((11, 3, 8, NX), F32),
            pltpu.VMEM((11, 3, 8, NX), F32),
            pltpu.VMEM((17, 3, 16, NX), F32),
            dma((8,)), dma((8,)), dma((8,)),
            dma((PIECES,)), dma((PIECES,)),
            dma((2 * PIECES,)), dma((2 * PIECES,)),
            dma((6,)), dma((6,)), dma((10,)), dma((10,)),
            dma((16,)), dma((16,)),
        ],
        compiler_params=pltpu.CompilerParams(
            collective_id=0, has_side_effects=True, vmem_limit_bytes=51 * 1024 * 1024
        ),
        cost_estimate=pl.CostEstimate(
            flops=60_000_000, bytes_accessed=8_000_000, transcendentals=400_000
        ),
    )(vol, attenuation.T, penalty, tv_weight)
    return out.reshape(3, 1, 256, NX)


def solution(mesh):
    placed = (P("bin", "slab", None, None), P(), P(), P())
    return jax.shard_map(
        on_device,
        mesh=mesh,
        in_specs=placed,
        out_specs=P(None, ("bin", "slab"), None, None),
        check_vma=False,
    )
```

```python
import jax
import jax.numpy as jnp
from jax import lax
from jax.experimental import pallas as pl
from jax.experimental.pallas import tpu as pltpu
from jax.sharding import PartitionSpec as P

MESH = pl.DeviceIdType.MESH
F32 = jnp.float32
HALO = 3
LAYERS = 16 + 2 * HALO
NX = 512
LAG = 4
PIECES = 16


def position():
    bin_index = lax.axis_index("bin")
    slab_index = lax.axis_index("slab")
    return (
        bin_index // 2,
        bin_index % 2,
        slab_index // 16,
        (slab_index // 8) % 2,
        (slab_index // 4) % 2,
        slab_index % 4,
    )


def device(xh, core, pz1, pz0, xl, py):
    return (xh * 2 + core, pz1 * 16 + pz0 * 8 + xl * 4 + py)


def block_device(zb, yb):
    pz0 = (zb // 2) % 2
    return device(zb // 4, yb % 2, yb // 8, pz0, (zb % 2) ^ pz0, (yb // 2) % 4)


def scalars(att, penalty, tv_weight, xh):
    rho = penalty[0]
    threshold = tv_weight[0] / rho
    gram = [[None] * 3 for _ in range(3)]
    for i in range(3):
        for j in range(i, 3):
            total = att[i, 0] * att[j, 0]
            for k in range(1, 8):
                total = total + att[i, k] * att[j, k]
            gram[i][j] = gram[j][i] = total + 12.0 * rho if i == j else total
    cofactor = [
        [
            gram[(r + 1) % 3][(c + 1) % 3] * gram[(r + 2) % 3][(c + 2) % 3]
            - gram[(r + 1) % 3][(c + 2) % 3] * gram[(r + 2) % 3][(c + 1) % 3]
            for c in range(3)
        ]
        for r in range(3)
    ]
    determinant = sum(gram[0][c] * cofactor[0][c] for c in range(3))
    inverse = [[cofactor[c][r] / determinant for c in range(3)] for r in range(3)]
    weight = [
        [sum(inverse[m][n] * att[n, 4 * xh + k] for n in range(3)) for k in range(4)]
        for m in range(3)
    ]
    scaled = [[rho * inverse[m][n] for n in range(3)] for m in range(3)]
    return threshold, weight, scaled


def kernel(
    vol, att, penalty, tv_weight, out,
    raw, part, passed, landed, base, field_one, field_two, dual_zero, dual_one, div_zero, div_one, carry,
    pack_lo, pack_hi, got_lo, got_hi, result,
    load_sem, core_send, core_recv, one_send, one_recv, two_send, two_recv,
    hz_send, hz_recv, hy_send, hy_recv, out_send, out_recv,
):
    xh, core, pz1, pz0, xl, py = position()
    turned_xl = xl ^ pz0
    zb = xh * 4 + pz0 * 2 + turned_xl
    yb = pz1 * 8 + py * 2 + core
    partner = device(xh, 1 - core, pz1, pz0, xl, py)
    across = device(xh, core, 1 - pz1, pz0, xl, py)

    def bins_at(n):
        return n // 2, pl.ds(((1 - n % 2) ^ pz1) * 4, 4)

    def load(n):
        layer, rows = bins_at(n)
        return pltpu.make_async_copy(
            vol.at[:, layer, rows, core], raw.at[pl.ds(core * 2, 2), layer, rows], load_sem.at[n]
        )

    def load_body(n, _):
        load(n).start()
        return 0

    lax.fori_loop(0, 8, load_body, 0)

    barrier = pltpu.get_barrier_semaphore()

    def greet(target):
        pl.semaphore_signal(barrier, inc=1, device_id=target, device_id_type=MESH)

    greet(partner)
    greet(across)
    for side in range(2):
        for row in range(4):
            target = device(side, core, pz1, pz0, turned_xl, row)

            @pl.when(jnp.logical_or(jnp.logical_or(side != xh, row != py), pz0 == 1))
            def _():
                greet(target)

    for dz in (1, 7):
        greet(block_device((zb + dz) % 8, yb))
    for dy in (1, 15):
        greet(block_device(zb, (yb + dy) % 16))

    home = jnp.logical_and(pz0 == core, pz1 == turned_xl)

    def greet_body(y, _):
        source = device(xh, y % 2, y // 8, core, pz1 ^ core, (y // 2) % 4)

        @pl.when(jnp.logical_not(jnp.logical_and(home, y == yb)))
        def _():
            greet(source)

        return 0

    lax.fori_loop(0, 16, greet_body, 0)

    threshold, weight, scaled = scalars(att, penalty, tv_weight, xh)

    @pl.when(zb == 0)
    def _():
        base[pl.ds(0, HALO)] = jnp.zeros((HALO, 3, 24, NX), F32)

    @pl.when(zb == 7)
    def _():
        base[pl.ds(16 + HALO, HALO)] = jnp.zeros((HALO, 3, 24, NX), F32)

    @pl.when(yb == 0)
    def _():
        got_lo[...] = jnp.zeros_like(got_lo)

    @pl.when(yb == 15)
    def _():
        got_hi[...] = jnp.zeros_like(got_hi)

    pl.semaphore_wait(barrier, 2 + 7 + pz0 + 4 + 16 - jnp.where(home, 1, 0))

    def swap(n):
        layer, rows = bins_at(n)
        return pltpu.make_async_remote_copy(
            src_ref=vol.at[:, layer, rows, 1 - core],
            dst_ref=raw.at[pl.ds(core * 2, 2), layer, rows],
            send_sem=core_send.at[n],
            recv_sem=core_recv.at[n],
            device_id=partner,
            device_id_type=MESH,
        )

    def swap_body(n, _):
        swap(n).start()
        return 0

    lax.fori_loop(0, 4, swap_body, 0)

    def project(n):
        load(n).wait()
        swap(n).wait_recv()

        @pl.when(n < 4)
        def _():
            swap(n + 4).start()

        layer = n // 2
        first = ((1 - n % 2) ^ pz1) * 4

        def body(k, _):
            q = first + k
            for r in range(2):
                rows = pl.ds(8 * r, 8)
                bins = [raw[b, layer, q, rows, :] for b in range(4)]
                for m in range(3):
                    part[q, layer, m, rows, :] = (
                        weight[m][0] * bins[0]
                        + weight[m][1] * bins[1]
                        + weight[m][2] * bins[2]
                        + weight[m][3] * bins[3]
                    )
            return 0

        lax.fori_loop(0, 4, body, 0)

    def ahead(i):
        k = i % 4
        return (jnp.where(k < 2, 2 * k + 1, 6 - 2 * k) + 2 * core) % 4

    def piece(i):
        return (py + ahead(i)) % 4, i // 4

    def one(i):
        row, h = piece(i)
        return pltpu.make_async_remote_copy(
            src_ref=part.at[(1 - pz1) * 4 + row, h],
            dst_ref=passed.at[row, h],
            send_sem=one_send.at[i],
            recv_sem=one_recv.at[i],
            device_id=across,
            device_id_type=MESH,
        )

    def two(i, passing):
        row, h = piece(i)
        source = passed.at[row, h] if passing else part.at[pz1 * 4 + row, h]
        return pltpu.make_async_remote_copy(
            src_ref=source,
            dst_ref=landed.at[xh, py, h],
            send_sem=two_send.at[i + PIECES * passing],
            recv_sem=two_recv.at[(xh * 4 + py) * 4 + h],
            device_id=device(1 - pz1 if passing else pz1, core, pz1, pz0, turned_xl, row),
            device_id_type=MESH,
        )

    def two_stays(i, passing):
        same = jnp.logical_and(xh == (1 - pz1 if passing else pz1), ahead(i) == 0)
        return jnp.logical_and(same, pz0 == 0)

    def two_start(i, passing):
        row, h = piece(i)
        stays = two_stays(i, passing)
        source = passed.at[row, h] if passing else part.at[pz1 * 4 + row, h]

        @pl.when(stays)
        def _():
            pltpu.make_async_copy(
                source, landed.at[xh, py, h], two_recv.at[(xh * 4 + py) * 4 + h]
            ).start()

        @pl.when(jnp.logical_not(stays))
        def _():
            two(i, passing).start()

    def two_sent(i, passing):
        @pl.when(jnp.logical_not(two_stays(i, passing)))
        def _():
            two(i, passing).wait_send()

    def pass_on(i):
        one(i).wait_recv()
        two_start(i, 1)

    def input_body(i, _):
        @pl.when(i % 4 == 0)
        def _():
            project(i // 2)
            project(i // 2 + 1)

        one(i).start()
        two_start(i, 0)

        @pl.when(i >= LAG)
        def _():
            pass_on(i - LAG)

        return 0

    lax.fori_loop(0, PIECES, input_body, 0)

    def tail_body(i, _):
        pass_on(i)
        return 0

    lax.fori_loop(PIECES - LAG, PIECES, tail_body, 0)

    below = block_device((zb + 7) % 8, yb)
    above = block_device((zb + 1) % 8, yb)
    before = block_device(zb, (yb + 15) % 16)
    after = block_device(zb, (yb + 1) % 16)
    has_below, has_above = zb > 0, zb < 7
    has_before, has_after = yb > 0, yb < 15

    def halo_z(which, n):
        first, target, place = ((HALO, below, 16 + HALO), (16, above, 0))[which]
        return pltpu.make_async_remote_copy(
            src_ref=base.at[first + n, :, pl.ds(0, 16)],
            dst_ref=base.at[place + n, :, pl.ds(0, 16)],
            send_sem=hz_send.at[which * 3 + n],
            recv_sem=hz_recv.at[which * 3 + n],
            device_id=target,
            device_id_type=MESH,
        )

    def halo_y(which, n):
        pack, got, target = ((pack_lo, got_hi, before), (pack_hi, got_lo, after))[which]
        late = isinstance(n, int) and n == 4
        rows = pl.ds(8, 3) if late else pl.ds(2 * n, 2)
        return pltpu.make_async_remote_copy(
            src_ref=pack.at[rows],
            dst_ref=got.at[rows],
            send_sem=hy_send.at[which * 5 + n],
            recv_sem=hy_recv.at[which * 5 + n],
            device_id=target,
            device_id_type=MESH,
        )

    sub = lax.broadcasted_iota(jnp.int32, (8, NX), 0)

    def pair(at, late):
        if late:
            return at - 8, at + 11
        first = HALO + at // 2 + 4 * (at % 2)
        return first, first + 8

    def pack_pair(at, late):
        first, second = pair(at, late)
        for m in range(3):
            lo_first = base[first, m, pl.ds(0, 8), :]
            lo_second = pltpu.roll(base[second, m, pl.ds(0, 8), :], 4, 0)
            pack_lo[at, m] = jnp.where(sub < 4, lo_first, lo_second)
            hi_first = base[first, m, pl.ds(8, 8), :]
            hi_second = pltpu.roll(base[second, m, pl.ds(8, 8), :], 4, 0)
            pack_hi[at, m] = jnp.where(sub < 4, hi_second, hi_first)

    def unpack_pair(at, late):
        first, second = pair(at, late)
        for m in range(3):
            lo = got_lo[at, m]
            hi = got_hi[at, m]
            base[first, m, pl.ds(16, 8), :] = jnp.where(sub < 4, hi, lo)
            base[second, m, pl.ds(16, 8), :] = pltpu.roll(jnp.where(sub < 4, lo, hi), 4, 0)

    def reduce_body(h, _):
        def piece_body(k, _):
            row = (py + 4 - ahead(k)) % 4
            for side in range(2):
                pltpu.make_async_remote_copy(
                    src_ref=landed.at[side, row, h],
                    dst_ref=landed.at[side, row, h],
                    send_sem=two_send.at[0],
                    recv_sem=two_recv.at[(side * 4 + row) * 4 + h],
                    device_id=partner,
                    device_id_type=MESH,
                ).wait_recv()
            layer = HALO + row * 4 + h
            for m in range(3):
                base[layer, m, pl.ds(0, 16), :] = landed[0, row, h, m] + landed[1, row, h, m]
            return 0

        lax.fori_loop(0, 4, piece_body, 0)

        @pl.when(jnp.logical_and(has_below, h < 3))
        def _():
            halo_z(0, h).start()

        @pl.when(jnp.logical_and(has_above, h > 0))
        def _():
            halo_z(1, h - 1).start()

        for half in range(2):
            pack_pair(2 * h + half, False)

        @pl.when(has_before)
        def _():
            halo_y(0, h).start()

        @pl.when(has_after)
        def _():
            halo_y(1, h).start()

        return 0

    lax.fori_loop(0, 4, reduce_body, 0)

    def arrive_y(n):
        @pl.when(has_after)
        def _():
            halo_y(0, n).wait_recv()

        @pl.when(has_before)
        def _():
            halo_y(1, n).wait_recv()

    def arrive_body(h, _):
        arrive_y(h)
        for half in range(2):
            unpack_pair(2 * h + half, False)
        return 0

    lax.fori_loop(0, 4, arrive_body, 0)

    lane = lax.broadcasted_iota(jnp.int32, (8, 128), 1)
    y_mask = {
        1: jnp.where(jnp.logical_and(sub == 7, yb == 15), 0.0, 1.0).astype(F32),
        2: jnp.where(jnp.logical_and(sub == 7, yb == 0), 0.0, 1.0).astype(F32),
    }
    limit = threshold * threshold

    def next_x(f):
        parts = [f[:, k : k + 128] for k in range(0, f.shape[1], 128)]
        turned = [pltpu.roll(p, 127, 1) for p in parts]
        later = turned[1:] + parts[-1:]
        return jnp.concatenate(
            [jnp.where(lane == 127, b, a) for a, b in zip(turned, later)], axis=1
        )

    def last_x(p):
        parts = [p[:, k : k + 128] for k in range(0, p.shape[1], 128)]
        turned = [pltpu.roll(q, 1, 1) for q in parts]
        earlier = [jnp.zeros_like(parts[0])] + turned[:-1]
        return jnp.concatenate(
            [jnp.where(lane == 0, b, a) for a, b in zip(turned, earlier)], axis=1
        )

    def sweep(turn, first, last, chain):
        src = (base, field_one, field_two)[turn]
        target = (field_one, field_two, result)[turn]
        dual = (dual_zero, dual_one, None)[turn]
        div = (div_zero, div_one, None)[turn]
        dual_past = (None, dual_zero, dual_one)[turn]
        div_past = (None, div_zero, div_one)[turn]

        def body(z, _):
            z_global = zb * 16 + z - HALO
            edge = jnp.logical_or(z_global == 127, z_global == -1)
            upper = z + jnp.where(edge, 0, 1)
            here = [[src[z, m, pl.ds(8 * t, 8), :] for m in range(3)] for t in range(3)]
            rolled = [[pltpu.roll(here[t][m], 7, 0) for m in range(3)] for t in range(3)]

            def duals(t):
                rows = pl.ds(8 * t, 8)
                values, squares = [], None
                for m in range(3):
                    f = here[t][m]
                    along_z = src[upper, m, rows, :] - f
                    along_y = jnp.where(sub == 7, rolled[(t + 1) % 3][m], rolled[t][m]) - f
                    if t:
                        along_y = along_y * y_mask[t]
                    along_x = next_x(f) - f
                    triple = [along_z, along_y, along_x]
                    if turn:
                        triple = [
                            triple[d] + dual_past[z, 3 * m + d, rows, :] for d in range(3)
                        ]
                    values.append(triple)
                    for v in triple:
                        squares = v * v if squares is None else squares + v * v
                scale = threshold * lax.rsqrt(jnp.maximum(squares, limit))
                fresh = [[v * scale for v in triple] for triple in values]
                if turn < 2:
                    for m in range(3):
                        for d in range(3):
                            dual[z, 3 * m + d, rows, :] = fresh[m][d]
                return fresh

            def inner(t, fresh):
                rows = pl.ds(8 * t, 8)
                partial, turned = [], []
                for m in range(3):
                    part_z, part_y, part_x = fresh[m]
                    total = part_z - carry[chain, turn, m, rows, :]
                    carry[chain, turn, m, rows, :] = part_z
                    partial.append(total + (part_x - last_x(part_x)) + part_y)
                    turned.append(pltpu.roll(part_y, 1, 0))
                return partial, turned

            def finish(t, partial, own, earlier):
                rows = pl.ds(8 * t, 8)
                total = []
                for m in range(3):
                    fresh_div = partial[m] - jnp.where(sub == 0, earlier[m], own[m])
                    if turn < 2:
                        div[z, m, rows, :] = fresh_div
                    step_div = fresh_div + fresh_div
                    if turn:
                        step_div = step_div - div_past[z, m, rows, :]
                    total.append(step_div + 12.0 * here[t][m])
                for m in range(3):
                    value = (
                        base[z, m, rows, :]
                        + scaled[m][0] * total[0]
                        + scaled[m][1] * total[1]
                        + scaled[m][2] * total[2]
                    )
                    target[z - 2 if turn == 2 else z, m, rows, :] = value

            fresh = duals(2)
            if turn < 2:
                partial_two, turned_two = inner(2, fresh)
            else:
                turned_two = [pltpu.roll(fresh[m][1], 1, 0) for m in range(3)]
            partial, turned_zero = inner(0, duals(0))
            finish(0, partial, turned_zero, turned_two)
            partial, turned_one = inner(1, duals(1))
            finish(1, partial, turned_one, turned_zero)
            if turn < 2:
                finish(2, partial_two, turned_two, turned_one)
            return 0

        lax.fori_loop(first, last + 1, body, 0)

    def send(layer):
        return pltpu.make_async_remote_copy(
            src_ref=result.at[1 + layer],
            dst_ref=out.at[:, pl.ds(pl.multiple_of(yb * 16, 16), 16)],
            send_sem=out_send.at[layer],
            recv_sem=out_recv.at[yb],
            device_id=(xh * 2 + pz0, turned_xl * 16 + layer),
            device_id_type=MESH,
        )

    own_layer = pz0 * 8 + xl * 4 + py

    def send_layer(layer):
        mine = jnp.logical_and(home, layer == own_layer)

        @pl.when(mine)
        def _():
            pltpu.make_async_copy(
                result.at[1 + layer],
                out.at[:, pl.ds(pl.multiple_of(yb * 16, 16), 16)],
                out_recv.at[yb],
            ).start()

        @pl.when(jnp.logical_not(mine))
        def _():
            send(layer).start()


    def layer_at(i):
        a, b = i % 4, i // 4
        low = (py + jnp.where(a < 2, 2 * a + 1, 6 - 2 * a) + 2 * core) % 4
        bit = xl ^ 1 ^ core ^ (b % 2)
        return low + 4 * bit + 8 * ((b // 2) ^ (a // 2) ^ pz1)

    def send_layers(first, last):
        def body(i, _):
            layer = layer_at(i)

            @pl.when(jnp.logical_and(layer >= first, layer <= last))
            def _():
                send_layer(layer)

            return 0

        lax.fori_loop(0, 16, body, 0)

    def either(zero, one):
        return jnp.where(core == 0, zero, one)

    sweep(0, either(3, 8), either(12, 17), 0)
    for n in range(3):
        @pl.when(has_above)
        def _():
            halo_z(0, n).wait_recv()

        @pl.when(has_below)
        def _():
            halo_z(1, n).wait_recv()

    for at in range(8, 11):
        pack_pair(at, True)

    @pl.when(has_before)
    def _():
        halo_y(0, 4).start()

    @pl.when(has_after)
    def _():
        halo_y(1, 4).start()

    sweep(1, either(4, 9), either(11, 16), 0)
    sweep(2, either(5, 10), either(10, 15), 0)
    send_layers(either(3, 8), either(7, 12))
    sweep(0, either(13, 3), either(17, 8), core)
    sweep(1, either(12, 4), either(16, 9), core)
    sweep(2, either(11, 5), either(15, 10), core)
    send_layers(either(8, 3), either(12, 7))
    arrive_y(4)
    for at in range(8, 11):
        unpack_pair(at, True)
    for half in range(2):
        upper = core == half
        for turn in range(3):
            sweep(
                turn,
                jnp.where(upper, 18 - turn, turn),
                jnp.where(upper, 20 - turn, 3 + turn),
                jnp.where(upper, 0, 1),
            )
        send_layers(jnp.where(upper, 13, 0), jnp.where(upper, 15, 2))

    def drain_swap(q, _):
        swap(q).wait_send()
        return 0

    lax.fori_loop(0, 8, drain_swap, 0)

    def drain_two(i, _):
        one(i).wait_send()
        two_sent(i, 0)
        two_sent(i, 1)
        return 0

    lax.fori_loop(0, PIECES, drain_two, 0)

    for which in range(2):
        @pl.when((has_below, has_above)[which])
        def _():
            for n in range(3):
                halo_z(which, n).wait_send()

        @pl.when((has_before, has_after)[which])
        def _():
            for n in range(5):
                halo_y(which, n).wait_send()

    def drain_out(i, _):
        @pl.when(jnp.logical_not(jnp.logical_and(home, i == own_layer)))
        def _():
            send(i).wait_send()

        pltpu.make_async_remote_copy(
            src_ref=result.at[0],
            dst_ref=out.at[:, pl.ds(pl.multiple_of(i * 16, 16), 16)],
            send_sem=out_send.at[0],
            recv_sem=out_recv.at[i],
            device_id=partner,
            device_id_type=MESH,
        ).wait_recv()
        return 0

    lax.fori_loop(0, 16, drain_out, 0)


def on_device(volumes, attenuation, penalty, tv_weight):
    vol = volumes.reshape(2, 4, 8, 2, 16, NX)
    dma = pltpu.SemaphoreType.DMA
    out = pl.pallas_call(
        kernel,
        out_shape=jax.ShapeDtypeStruct((3, 256, NX), F32),
        in_specs=[pl.BlockSpec(memory_space=pl.ANY)]
        + [pl.BlockSpec(memory_space=pltpu.SMEM)] * 3,
        out_specs=pl.BlockSpec(memory_space=pl.ANY),
        scratch_shapes=[
            pltpu.VMEM((4, 4, 8, 16, NX), F32),
            pltpu.VMEM((8, 4, 3, 16, NX), F32),
            pltpu.VMEM((4, 4, 3, 16, NX), F32),
            pltpu.VMEM((2, 4, 4, 3, 16, NX), F32),
            pltpu.VMEM((LAYERS, 3, 24, NX), F32),
            pltpu.VMEM((LAYERS, 3, 24, NX), F32),
            pltpu.VMEM((LAYERS, 3, 24, NX), F32),
            pltpu.VMEM((LAYERS, 9, 24, NX), F32),
            pltpu.VMEM((LAYERS, 9, 24, NX), F32),
            pltpu.VMEM((LAYERS, 3, 24, NX), F32),
            pltpu.VMEM((LAYERS, 3, 24, NX), F32),
            pltpu.VMEM((2, 3, 3, 24, NX), F32),
            pltpu.VMEM((11, 3, 8, NX), F32),
            pltpu.VMEM((11, 3, 8, NX), F32),
            pltpu.VMEM((11, 3, 8, NX), F32),
            pltpu.VMEM((11, 3, 8, NX), F32),
            pltpu.VMEM((17, 3, 16, NX), F32),
            dma((8,)), dma((8,)), dma((8,)),
            dma((PIECES,)), dma((PIECES,)),
            dma((2 * PIECES,)), dma((2 * PIECES,)),
            dma((6,)), dma((6,)), dma((10,)), dma((10,)),
            dma((16,)), dma((16,)),
        ],
        compiler_params=pltpu.CompilerParams(
            collective_id=0, has_side_effects=True, vmem_limit_bytes=51 * 1024 * 1024
        ),
        cost_estimate=pl.CostEstimate(
            flops=60_000_000, bytes_accessed=8_000_000, transcendentals=400_000
        ),
    )(vol, attenuation.T, penalty, tv_weight)
    return out.reshape(3, 1, 256, NX)


def solution(mesh):
    placed = (P("bin", "slab", None, None), P(), P(), P())
    return jax.shard_map(
        on_device,
        mesh=mesh,
        in_specs=placed,
        out_specs=P(None, ("bin", "slab"), None, None),
        check_vma=False,
    )
```

```python
import jax
import jax.numpy as jnp
from jax import lax
from jax.experimental import pallas as pl
from jax.experimental.pallas import tpu as pltpu
from jax.sharding import PartitionSpec as P

MESH = pl.DeviceIdType.MESH
F32 = jnp.float32
HALO = 3
LAYERS = 16 + 2 * HALO
NX = 512
LAG = 4
PIECES = 16


def position():
    bin_index = lax.axis_index("bin")
    slab_index = lax.axis_index("slab")
    return (
        bin_index // 2,
        bin_index % 2,
        slab_index // 16,
        (slab_index // 8) % 2,
        (slab_index // 4) % 2,
        slab_index % 4,
    )


def device(xh, core, pz1, pz0, xl, py):
    return (xh * 2 + core, pz1 * 16 + pz0 * 8 + xl * 4 + py)


def block_device(zb, yb):
    pz0 = (zb // 2) % 2
    return device(zb // 4, yb % 2, yb // 8, pz0, (zb % 2) ^ pz0, (yb // 2) % 4)


def scalars(att, penalty, tv_weight, xh):
    rho = penalty[0]
    threshold = tv_weight[0] / rho
    gram = [[None] * 3 for _ in range(3)]
    for i in range(3):
        for j in range(i, 3):
            total = att[i, 0] * att[j, 0]
            for k in range(1, 8):
                total = total + att[i, k] * att[j, k]
            gram[i][j] = gram[j][i] = total + 12.0 * rho if i == j else total
    cofactor = [
        [
            gram[(r + 1) % 3][(c + 1) % 3] * gram[(r + 2) % 3][(c + 2) % 3]
            - gram[(r + 1) % 3][(c + 2) % 3] * gram[(r + 2) % 3][(c + 1) % 3]
            for c in range(3)
        ]
        for r in range(3)
    ]
    determinant = sum(gram[0][c] * cofactor[0][c] for c in range(3))
    inverse = [[cofactor[c][r] / determinant for c in range(3)] for r in range(3)]
    weight = [
        [sum(inverse[m][n] * att[n, 4 * xh + k] for n in range(3)) for k in range(4)]
        for m in range(3)
    ]
    scaled = [[rho * inverse[m][n] for n in range(3)] for m in range(3)]
    return threshold, weight, scaled


def kernel(
    vol, att, penalty, tv_weight, out,
    raw, part, passed, landed, base, field_one, field_two, dual_zero, dual_one, div_zero, div_one, carry,
    pack_lo, pack_hi, got_lo, got_hi, result,
    load_sem, core_send, core_recv, one_send, one_recv, two_send, two_recv,
    hz_send, hz_recv, hy_send, hy_recv, out_send, out_recv,
):
    xh, core, pz1, pz0, xl, py = position()
    turned_xl = xl ^ pz0
    zb = xh * 4 + pz0 * 2 + turned_xl
    yb = pz1 * 8 + py * 2 + core
    partner = device(xh, 1 - core, pz1, pz0, xl, py)
    across = device(xh, core, 1 - pz1, pz0, xl, py)

    def bins_at(n):
        return n // 2, pl.ds(((1 - n % 2) ^ pz1) * 4, 4)

    def load(n):
        layer, rows = bins_at(n)
        return pltpu.make_async_copy(
            vol.at[:, layer, rows, core], raw.at[pl.ds(core * 2, 2), layer, rows], load_sem.at[n]
        )

    def load_body(n, _):
        load(n).start()
        return 0

    lax.fori_loop(0, 8, load_body, 0)

    barrier = pltpu.get_barrier_semaphore()

    def greet(target):
        pl.semaphore_signal(barrier, inc=1, device_id=target, device_id_type=MESH)

    greet(partner)
    greet(across)
    for side in range(2):
        for row in range(4):
            target = device(side, core, pz1, pz0, turned_xl, row)

            @pl.when(jnp.logical_or(jnp.logical_or(side != xh, row != py), pz0 == 1))
            def _():
                greet(target)

    for dz in (1, 7):
        greet(block_device((zb + dz) % 8, yb))
    for dy in (1, 15):
        greet(block_device(zb, (yb + dy) % 16))

    home = jnp.logical_and(pz0 == core, pz1 == turned_xl)

    def greet_body(y, _):
        source = device(xh, y % 2, y // 8, core, pz1 ^ core, (y // 2) % 4)

        @pl.when(jnp.logical_not(jnp.logical_and(home, y == yb)))
        def _():
            greet(source)

        return 0

    lax.fori_loop(0, 16, greet_body, 0)

    threshold, weight, scaled = scalars(att, penalty, tv_weight, xh)

    @pl.when(zb == 0)
    def _():
        base[pl.ds(0, HALO)] = jnp.zeros((HALO, 3, 24, NX), F32)

    @pl.when(zb == 7)
    def _():
        base[pl.ds(16 + HALO, HALO)] = jnp.zeros((HALO, 3, 24, NX), F32)

    @pl.when(yb == 0)
    def _():
        got_lo[...] = jnp.zeros_like(got_lo)

    @pl.when(yb == 15)
    def _():
        got_hi[...] = jnp.zeros_like(got_hi)

    pl.semaphore_wait(barrier, 2 + 7 + pz0 + 4 + 16 - jnp.where(home, 1, 0))

    def swap(n):
        layer, rows = bins_at(n)
        return pltpu.make_async_remote_copy(
            src_ref=vol.at[:, layer, rows, 1 - core],
            dst_ref=raw.at[pl.ds(core * 2, 2), layer, rows],
            send_sem=core_send.at[n],
            recv_sem=core_recv.at[n],
            device_id=partner,
            device_id_type=MESH,
        )

    def swap_body(n, _):
        swap(n).start()
        return 0

    lax.fori_loop(0, 4, swap_body, 0)

    def project(n):
        load(n).wait()
        swap(n).wait_recv()

        @pl.when(n < 4)
        def _():
            swap(n + 4).start()

        layer = n // 2
        first = ((1 - n % 2) ^ pz1) * 4

        def body(k, _):
            q = first + k
            for r in range(2):
                rows = pl.ds(8 * r, 8)
                bins = [raw[b, layer, q, rows, :] for b in range(4)]
                for m in range(3):
                    part[q, layer, m, rows, :] = (
                        weight[m][0] * bins[0]
                        + weight[m][1] * bins[1]
                        + weight[m][2] * bins[2]
                        + weight[m][3] * bins[3]
                    )
            return 0

        lax.fori_loop(0, 4, body, 0)

    def ahead(i):
        k = i % 4
        return (jnp.where(k < 2, 2 * k + 1, 6 - 2 * k) + 2 * core) % 4

    def piece(i):
        return (py + ahead(i)) % 4, i // 4

    def one(i):
        row, h = piece(i)
        return pltpu.make_async_remote_copy(
            src_ref=part.at[(1 - pz1) * 4 + row, h],
            dst_ref=passed.at[row, h],
            send_sem=one_send.at[i],
            recv_sem=one_recv.at[i],
            device_id=across,
            device_id_type=MESH,
        )

    def two(i, passing):
        row, h = piece(i)
        source = passed.at[row, h] if passing else part.at[pz1 * 4 + row, h]
        return pltpu.make_async_remote_copy(
            src_ref=source,
            dst_ref=landed.at[xh, py, h],
            send_sem=two_send.at[i + PIECES * passing],
            recv_sem=two_recv.at[(xh * 4 + py) * 4 + h],
            device_id=device(1 - pz1 if passing else pz1, core, pz1, pz0, turned_xl, row),
            device_id_type=MESH,
        )

    def two_stays(i, passing):
        same = jnp.logical_and(xh == (1 - pz1 if passing else pz1), ahead(i) == 0)
        return jnp.logical_and(same, pz0 == 0)

    def two_start(i, passing):
        row, h = piece(i)
        stays = two_stays(i, passing)
        source = passed.at[row, h] if passing else part.at[pz1 * 4 + row, h]

        @pl.when(stays)
        def _():
            pltpu.make_async_copy(
                source, landed.at[xh, py, h], two_recv.at[(xh * 4 + py) * 4 + h]
            ).start()

        @pl.when(jnp.logical_not(stays))
        def _():
            two(i, passing).start()

    def two_sent(i, passing):
        @pl.when(jnp.logical_not(two_stays(i, passing)))
        def _():
            two(i, passing).wait_send()

    def pass_on(i):
        one(i).wait_recv()
        two_start(i, 1)

    def input_body(i, _):
        @pl.when(i % 4 == 0)
        def _():
            project(i // 2)
            project(i // 2 + 1)

        one(i).start()
        two_start(i, 0)

        @pl.when(i >= LAG)
        def _():
            pass_on(i - LAG)

        return 0

    lax.fori_loop(0, PIECES, input_body, 0)

    def tail_body(i, _):
        pass_on(i)
        return 0

    lax.fori_loop(PIECES - LAG, PIECES, tail_body, 0)

    below = block_device((zb + 7) % 8, yb)
    above = block_device((zb + 1) % 8, yb)
    before = block_device(zb, (yb + 15) % 16)
    after = block_device(zb, (yb + 1) % 16)
    has_below, has_above = zb > 0, zb < 7
    has_before, has_after = yb > 0, yb < 15

    def halo_z(which, n):
        first, target, place = ((HALO, below, 16 + HALO), (16, above, 0))[which]
        return pltpu.make_async_remote_copy(
            src_ref=base.at[first + n, :, pl.ds(0, 16)],
            dst_ref=base.at[place + n, :, pl.ds(0, 16)],
            send_sem=hz_send.at[which * 3 + n],
            recv_sem=hz_recv.at[which * 3 + n],
            device_id=target,
            device_id_type=MESH,
        )

    def halo_y(which, n):
        pack, got, target = ((pack_lo, got_hi, before), (pack_hi, got_lo, after))[which]
        late = isinstance(n, int) and n == 4
        rows = pl.ds(8, 3) if late else pl.ds(2 * n, 2)
        return pltpu.make_async_remote_copy(
            src_ref=pack.at[rows],
            dst_ref=got.at[rows],
            send_sem=hy_send.at[which * 5 + n],
            recv_sem=hy_recv.at[which * 5 + n],
            device_id=target,
            device_id_type=MESH,
        )

    sub = lax.broadcasted_iota(jnp.int32, (8, NX), 0)

    def pair(at, late):
        if late:
            return at - 8, at + 11
        first = HALO + at // 2 + 4 * (at % 2)
        return first, first + 8

    def pack_pair(at, late):
        first, second = pair(at, late)
        for m in range(3):
            lo_first = base[first, m, pl.ds(0, 8), :]
            lo_second = pltpu.roll(base[second, m, pl.ds(0, 8), :], 4, 0)
            pack_lo[at, m] = jnp.where(sub < 4, lo_first, lo_second)
            hi_first = base[first, m, pl.ds(8, 8), :]
            hi_second = pltpu.roll(base[second, m, pl.ds(8, 8), :], 4, 0)
            pack_hi[at, m] = jnp.where(sub < 4, hi_second, hi_first)

    def unpack_pair(at, late):
        first, second = pair(at, late)
        for m in range(3):
            lo = got_lo[at, m]
            hi = got_hi[at, m]
            base[first, m, pl.ds(16, 8), :] = jnp.where(sub < 4, hi, lo)
            base[second, m, pl.ds(16, 8), :] = pltpu.roll(jnp.where(sub < 4, lo, hi), 4, 0)

    def reduce_body(h, _):
        def piece_body(k, _):
            row = (py + 4 - ahead(k)) % 4
            for side in range(2):
                pltpu.make_async_remote_copy(
                    src_ref=landed.at[side, row, h],
                    dst_ref=landed.at[side, row, h],
                    send_sem=two_send.at[0],
                    recv_sem=two_recv.at[(side * 4 + row) * 4 + h],
                    device_id=partner,
                    device_id_type=MESH,
                ).wait_recv()
            layer = HALO + row * 4 + h
            for m in range(3):
                base[layer, m, pl.ds(0, 16), :] = landed[0, row, h, m] + landed[1, row, h, m]
            return 0

        lax.fori_loop(0, 4, piece_body, 0)

        @pl.when(jnp.logical_and(has_below, h < 3))
        def _():
            halo_z(0, h).start()

        @pl.when(jnp.logical_and(has_above, h > 0))
        def _():
            halo_z(1, h - 1).start()

        for half in range(2):
            pack_pair(2 * h + half, False)

        @pl.when(has_before)
        def _():
            halo_y(0, h).start()

        @pl.when(has_after)
        def _():
            halo_y(1, h).start()

        return 0

    lax.fori_loop(0, 4, reduce_body, 0)

    def arrive_y(n):
        @pl.when(has_after)
        def _():
            halo_y(0, n).wait_recv()

        @pl.when(has_before)
        def _():
            halo_y(1, n).wait_recv()

    def arrive_body(h, _):
        arrive_y(h)
        for half in range(2):
            unpack_pair(2 * h + half, False)
        return 0

    lax.fori_loop(0, 4, arrive_body, 0)

    lane = lax.broadcasted_iota(jnp.int32, (8, 128), 1)
    y_mask = {
        1: jnp.where(jnp.logical_and(sub == 7, yb == 15), 0.0, 1.0).astype(F32),
        2: jnp.where(jnp.logical_and(sub == 7, yb == 0), 0.0, 1.0).astype(F32),
    }
    limit = threshold * threshold

    def next_x(f):
        parts = [f[:, k : k + 128] for k in range(0, f.shape[1], 128)]
        turned = [pltpu.roll(p, 127, 1) for p in parts]
        later = turned[1:] + parts[-1:]
        return jnp.concatenate(
            [jnp.where(lane == 127, b, a) for a, b in zip(turned, later)], axis=1
        )

    def last_x(p):
        parts = [p[:, k : k + 128] for k in range(0, p.shape[1], 128)]
        turned = [pltpu.roll(q, 1, 1) for q in parts]
        earlier = [jnp.zeros_like(parts[0])] + turned[:-1]
        return jnp.concatenate(
            [jnp.where(lane == 0, b, a) for a, b in zip(turned, earlier)], axis=1
        )

    def sweep(turn, first, last, chain):
        src = (base, field_one, field_two)[turn]
        target = (field_one, field_two, result)[turn]
        dual = (dual_zero, dual_one, None)[turn]
        div = (div_zero, div_one, None)[turn]
        dual_past = (None, dual_zero, dual_one)[turn]
        div_past = (None, div_zero, div_one)[turn]

        def body(z, _):
            z_global = zb * 16 + z - HALO
            edge = jnp.logical_or(z_global == 127, z_global == -1)
            upper = z + jnp.where(edge, 0, 1)
            here = [[src[z, m, pl.ds(8 * t, 8), :] for m in range(3)] for t in range(3)]
            rolled = [[pltpu.roll(here[t][m], 7, 0) for m in range(3)] for t in range(3)]

            def duals(t):
                rows = pl.ds(8 * t, 8)
                values, squares = [], None
                for m in range(3):
                    f = here[t][m]
                    along_z = src[upper, m, rows, :] - f
                    along_y = jnp.where(sub == 7, rolled[(t + 1) % 3][m], rolled[t][m]) - f
                    if t:
                        along_y = along_y * y_mask[t]
                    along_x = next_x(f) - f
                    triple = [along_z, along_y, along_x]
                    if turn:
                        triple = [
                            triple[d] + dual_past[z, 3 * m + d, rows, :] for d in range(3)
                        ]
                    values.append(triple)
                    for v in triple:
                        squares = v * v if squares is None else squares + v * v
                scale = threshold * lax.rsqrt(jnp.maximum(squares, limit))
                fresh = [[v * scale for v in triple] for triple in values]
                if turn < 2:
                    for m in range(3):
                        for d in range(3):
                            dual[z, 3 * m + d, rows, :] = fresh[m][d]
                return fresh

            def inner(t, fresh):
                rows = pl.ds(8 * t, 8)
                partial, turned = [], []
                for m in range(3):
                    part_z, part_y, part_x = fresh[m]
                    total = part_z - carry[chain, turn, m, rows, :]
                    carry[chain, turn, m, rows, :] = part_z
                    partial.append(total + (part_x - last_x(part_x)) + part_y)
                    turned.append(pltpu.roll(part_y, 1, 0))
                return partial, turned

            def finish(t, partial, own, earlier):
                rows = pl.ds(8 * t, 8)
                total = []
                for m in range(3):
                    fresh_div = partial[m] - jnp.where(sub == 0, earlier[m], own[m])
                    if turn < 2:
                        div[z, m, rows, :] = fresh_div
                    step_div = fresh_div + fresh_div
                    if turn:
                        step_div = step_div - div_past[z, m, rows, :]
                    total.append(step_div + 12.0 * here[t][m])
                for m in range(3):
                    value = (
                        base[z, m, rows, :]
                        + scaled[m][0] * total[0]
                        + scaled[m][1] * total[1]
                        + scaled[m][2] * total[2]
                    )
                    target[z - 2 if turn == 2 else z, m, rows, :] = value

            fresh = duals(2)
            if turn < 2:
                partial_two, turned_two = inner(2, fresh)
            else:
                turned_two = [pltpu.roll(fresh[m][1], 1, 0) for m in range(3)]
            partial, turned_zero = inner(0, duals(0))
            finish(0, partial, turned_zero, turned_two)
            partial, turned_one = inner(1, duals(1))
            finish(1, partial, turned_one, turned_zero)
            if turn < 2:
                finish(2, partial_two, turned_two, turned_one)
            return 0

        lax.fori_loop(first, last + 1, body, 0)

    def send(layer):
        return pltpu.make_async_remote_copy(
            src_ref=result.at[1 + layer],
            dst_ref=out.at[:, pl.ds(pl.multiple_of(yb * 16, 16), 16)],
            send_sem=out_send.at[layer],
            recv_sem=out_recv.at[yb],
            device_id=(xh * 2 + pz0, turned_xl * 16 + layer),
            device_id_type=MESH,
        )

    own_layer = pz0 * 8 + xl * 4 + py

    def send_layer(layer):
        mine = jnp.logical_and(home, layer == own_layer)

        @pl.when(mine)
        def _():
            pltpu.make_async_copy(
                result.at[1 + layer],
                out.at[:, pl.ds(pl.multiple_of(yb * 16, 16), 16)],
                out_recv.at[yb],
            ).start()

        @pl.when(jnp.logical_not(mine))
        def _():
            send(layer).start()


    def layer_at(i):
        a, b = i % 4, i // 4
        low = (py + jnp.where(a < 2, 2 * a + 1, 6 - 2 * a) + 2 * core) % 4
        bit = xl ^ 1 ^ core ^ (b % 2)
        return low + 4 * bit + 8 * ((b // 2) ^ (a // 2) ^ pz1)

    def send_layers(first, last):
        def body(i, _):
            layer = layer_at(i)

            @pl.when(jnp.logical_and(layer >= first, layer <= last))
            def _():
                send_layer(layer)

            return 0

        lax.fori_loop(0, 16, body, 0)

    def either(zero, one):
        return jnp.where(core == 0, zero, one)

    sweep(0, either(3, 8), either(12, 17), 0)
    sweep(1, either(4, 9), either(11, 16), 0)
    for n in range(3):
        @pl.when(has_above)
        def _():
            halo_z(0, n).wait_recv()

        @pl.when(has_below)
        def _():
            halo_z(1, n).wait_recv()

    for at in range(8, 11):
        pack_pair(at, True)

    @pl.when(has_before)
    def _():
        halo_y(0, 4).start()

    @pl.when(has_after)
    def _():
        halo_y(1, 4).start()

    sweep(2, either(5, 10), either(10, 15), 0)
    send_layers(either(3, 8), either(7, 12))
    sweep(0, either(13, 3), either(17, 8), core)
    sweep(1, either(12, 4), either(16, 9), core)
    sweep(2, either(11, 5), either(15, 10), core)
    send_layers(either(8, 3), either(12, 7))
    arrive_y(4)
    for at in range(8, 11):
        unpack_pair(at, True)
    for half in range(2):
        upper = core == half
        for turn in range(3):
            sweep(
                turn,
                jnp.where(upper, 18 - turn, turn),
                jnp.where(upper, 20 - turn, 3 + turn),
                jnp.where(upper, 0, 1),
            )
        send_layers(jnp.where(upper, 13, 0), jnp.where(upper, 15, 2))

    def drain_swap(q, _):
        swap(q).wait_send()
        return 0

    lax.fori_loop(0, 8, drain_swap, 0)

    def drain_two(i, _):
        one(i).wait_send()
        two_sent(i, 0)
        two_sent(i, 1)
        return 0

    lax.fori_loop(0, PIECES, drain_two, 0)

    for which in range(2):
        @pl.when((has_below, has_above)[which])
        def _():
            for n in range(3):
                halo_z(which, n).wait_send()

        @pl.when((has_before, has_after)[which])
        def _():
            for n in range(5):
                halo_y(which, n).wait_send()

    def drain_out(i, _):
        @pl.when(jnp.logical_not(jnp.logical_and(home, i == own_layer)))
        def _():
            send(i).wait_send()

        pltpu.make_async_remote_copy(
            src_ref=result.at[0],
            dst_ref=out.at[:, pl.ds(pl.multiple_of(i * 16, 16), 16)],
            send_sem=out_send.at[0],
            recv_sem=out_recv.at[i],
            device_id=partner,
            device_id_type=MESH,
        ).wait_recv()
        return 0

    lax.fori_loop(0, 16, drain_out, 0)


def on_device(volumes, attenuation, penalty, tv_weight):
    vol = volumes.reshape(2, 4, 8, 2, 16, NX)
    dma = pltpu.SemaphoreType.DMA
    out = pl.pallas_call(
        kernel,
        out_shape=jax.ShapeDtypeStruct((3, 256, NX), F32),
        in_specs=[pl.BlockSpec(memory_space=pl.ANY)]
        + [pl.BlockSpec(memory_space=pltpu.SMEM)] * 3,
        out_specs=pl.BlockSpec(memory_space=pl.ANY),
        scratch_shapes=[
            pltpu.VMEM((4, 4, 8, 16, NX), F32),
            pltpu.VMEM((8, 4, 3, 16, NX), F32),
            pltpu.VMEM((4, 4, 3, 16, NX), F32),
            pltpu.VMEM((2, 4, 4, 3, 16, NX), F32),
            pltpu.VMEM((LAYERS, 3, 24, NX), F32),
            pltpu.VMEM((LAYERS, 3, 24, NX), F32),
            pltpu.VMEM((LAYERS, 3, 24, NX), F32),
            pltpu.VMEM((LAYERS, 9, 24, NX), F32),
            pltpu.VMEM((LAYERS, 9, 24, NX), F32),
            pltpu.VMEM((LAYERS, 3, 24, NX), F32),
            pltpu.VMEM((LAYERS, 3, 24, NX), F32),
            pltpu.VMEM((2, 3, 3, 24, NX), F32),
            pltpu.VMEM((11, 3, 8, NX), F32),
            pltpu.VMEM((11, 3, 8, NX), F32),
            pltpu.VMEM((11, 3, 8, NX), F32),
            pltpu.VMEM((11, 3, 8, NX), F32),
            pltpu.VMEM((17, 3, 16, NX), F32),
            dma((8,)), dma((8,)), dma((8,)),
            dma((PIECES,)), dma((PIECES,)),
            dma((2 * PIECES,)), dma((2 * PIECES,)),
            dma((6,)), dma((6,)), dma((10,)), dma((10,)),
            dma((16,)), dma((16,)),
        ],
        compiler_params=pltpu.CompilerParams(
            collective_id=0, has_side_effects=True, vmem_limit_bytes=51 * 1024 * 1024
        ),
        cost_estimate=pl.CostEstimate(
            flops=60_000_000, bytes_accessed=8_000_000, transcendentals=400_000
        ),
    )(vol, attenuation.T, penalty, tv_weight)
    return out.reshape(3, 1, 256, NX)


def solution(mesh):
    placed = (P("bin", "slab", None, None), P(), P(), P())
    return jax.shard_map(
        on_device,
        mesh=mesh,
        in_specs=placed,
        out_specs=P(None, ("bin", "slab"), None, None),
        check_vma=False,
    )
```
